32 devices in a mesh: dp: 4 (over y, x), ctx: 8 (over z, core).
Axes of the slice: x: 2, y: 2, z: 4, core: 2. Of those that a mesh axis runs over, the one named last changes fastest.
Arguments:
- tokens: bfloat16 [4, 1536, 2048], P('dp', 'ctx'), may hold values from -6 to 6
- prefix: int32 [4], P('dp'), may hold values from 153 to 768
- g_attn: bfloat16 [2048], P(('dp', 'ctx')), may hold values from 0.099609375 to 1.8984375
- w_query: bfloat16 [2048, 2048], P(('dp', 'ctx')), may hold values from -0.125 to 0.125
- w_key: bfloat16 [2048, 1024], P(('dp', 'ctx')), may hold values from -0.125 to 0.125
- w_value: bfloat16 [2048, 1024], P(('dp', 'ctx')), may hold values from -0.125 to 0.125
- w_output: bfloat16 [2048, 2048], P(('dp', 'ctx')), may hold values from -3 to 3
- g_mlp: bfloat16 [2048], P(('dp', 'ctx')), may hold values from 0.099609375 to 1.8984375
- w_gate: bfloat16 [2048, 8192], P(('dp', 'ctx')), may hold values from -0.125 to 0.125
- w_up: bfloat16 [2048, 8192], P(('dp', 'ctx')), may hold values from -0.125 to 0.125
- w_down: bfloat16 [8192, 2048], P(('dp', 'ctx')), may hold values from -0.0625 to 0.0625
- cotangent: bfloat16 [4, 1536, 2048], P('dp', 'ctx'), may hold values from -6 to 6
Outputs:
- out: bfloat16 [4, 1536, 2048], P('dp', 'ctx')
- input_grad: bfloat16 [4, 1536, 2048], P('dp', 'ctx')
- grad_g_attn: float32 [2048], P(('dp', 'ctx'))
- grad_query: float32 [2048, 2048], P(('dp', 'ctx'))
- grad_key: float32 [2048, 1024], P(('dp', 'ctx'))
- grad_value: float32 [2048, 1024], P(('dp', 'ctx'))
- grad_output: float32 [2048, 2048], P(('dp', 'ctx'))
- grad_g_mlp: float32 [2048], P(('dp', 'ctx'))
- grad_gate: float32 [2048, 8192], P(('dp', 'ctx'))
- grad_up: float32 [2048, 8192], P(('dp', 'ctx'))
- grad_down: float32 [8192, 2048], P(('dp', 'ctx'))
The draws below stay inside these ranges and needn't reach their ends.
All inputs are finite; a program needn't handle non-finite values.
Results may differ from the reference program's by a relative error of at most 0.018.
Values may be sent and summed in bfloat16 or wider, within the bound.
No kernel may reach another device: no remote copies, remote signals or barrier semaphores. Data moves between devices by JAX's collectives and lax.ppermute only.
A program may use at most 704 MiB of HBM per device.

```python
import jax
import jax.numpy as jnp
from jax import lax

D = 2048
FF = 8192
H = 8
KVH = 4
HD = 256
QW = 2048
KW = 1024
LEN = 1536
SEQS = 4


def plant(values, rng, least, top_value):
    longest = values.shape.index(max(values.shape))
    spots = []
    for shift in (0, 1):
        where = [jax.random.randint(jax.random.fold_in(rng, axis), (), 0, length) for axis, length in enumerate(values.shape)]
        where[longest] = (where[longest] + shift) % values.shape[longest]
        spots.append(tuple(where))
    return values.at[spots[0]].set(least).at[spots[1]].set(top_value)


def block_levels(stream_key, extent, pieces, smallest, largest):
    gain, own = 1.0, jax.random.fold_in(stream_key, 6)
    for position, shards_of in pieces:
        heights = jnp.exp(jax.random.uniform(jax.random.fold_in(own, position), (shards_of,), jnp.float32, smallest / len(pieces), largest / len(pieces)))
        gain = gain * jnp.repeat(heights, extent[position] // shards_of).reshape([-1 if axis == position else 1 for axis in range(len(extent))])
    return gain


def centred(rng, dims, spread, reach, pieces=(), held_as=jnp.bfloat16):
    gain = block_levels(rng, dims, pieces, -0.22, 0.18) if pieces else 1.0
    array = jax.random.normal(rng, dims, jnp.float32) * spread * gain
    return jnp.minimum(jnp.maximum(array, -reach), reach).astype(held_as)


def setup_inputs(seed: int = 0) -> dict:
    splits = jax.random.split(jax.random.key(seed), 13)
    tokens = centred(splits[0], (SEQS, LEN, D), 1.0, 6.0, ((0, 4), (1, 8)))
    prefix = plant(jax.random.randint(splits[1], (SEQS,), LEN // 10, LEN // 2 + 1), jax.random.fold_in(splits[1], 1), LEN // 10, (LEN // 2 + 1) - 1).astype(jnp.int32)
    g_attn = jnp.clip(1.0 + 0.18 * jax.random.normal(splits[2], (D,), jnp.float32), 0.099609375, 1.8984375).astype(jnp.bfloat16)
    w_query = centred(splits[3], (D, QW), D ** -0.5, 0.125, ((0, 32),))
    w_key = centred(splits[4], (D, KW), D ** -0.5, 0.125, ((0, 32),))
    w_value = centred(splits[5], (D, KW), D ** -0.5, 0.125, ((0, 32),))
    w_output = centred(splits[6], (QW, D), 4 ** -0.5, 3.0, ((0, 32),))
    g_mlp = jnp.clip(1.0 + 0.18 * jax.random.normal(splits[7], (D,), jnp.float32), 0.099609375, 1.8984375).astype(jnp.bfloat16)
    w_gate = centred(splits[8], (D, FF), D ** -0.5, 0.125, ((0, 32),))
    w_up = centred(splits[9], (D, FF), D ** -0.5, 0.125, ((0, 32),))
    w_down = centred(splits[10], (FF, D), FF ** -0.5, 0.0625, ((0, 32),))
    cotangent = centred(splits[11], (SEQS, LEN, D), 1.0, 6.0, ((0, 4), (1, 8)))
    return {"tokens": tokens, "prefix": prefix, "g_attn": g_attn, "w_query": w_query, "w_key": w_key, "w_value": w_value, "w_output": w_output, "g_mlp": g_mlp, "w_gate": w_gate, "w_up": w_up, "w_down": w_down, "cotangent": cotangent}


EPS = 1e-06
THETA = 1000042.0
NEG = -1e+30
HIGH = lax.Precision.HIGHEST

@jax.custom_vjp
def low(v):
    return lax.optimization_barrier(v.astype(jnp.bfloat16)).astype(jnp.float32)

@jax.custom_vjp
def low_back(v):
    return v

def low_keep(v):
    return (low(v), None)

def low_pass(kept, grad):
    return (grad,)

def back_keep(v):
    return (v, None)

def back_low(kept, grad):
    return (low(grad),)
low.defvjp(low_keep, low_pass)
low_back.defvjp(back_keep, back_low)

def normalize(values):
    return values * lax.rsqrt(lax.optimization_barrier(jnp.mean(values * values, axis=-1, keepdims=True)) + EPS)

def rotary(first_pos, length, head_dim):
    half_dim = head_dim // 2
    frequency = 1.0 / THETA ** (lax.iota(jnp.float32, half_dim) * (2.0 / head_dim))
    angles = (first_pos + lax.iota(jnp.int32, length)).astype(jnp.float32)[:, None] * frequency[None, :]
    cosine = jnp.concatenate((jnp.cos(angles), jnp.cos(angles)), axis=1)
    sine_table = jnp.concatenate((jnp.sin(angles), jnp.sin(angles)), axis=1)
    return (cosine, sine_table)

def rotate(values, cosine, sine_table):
    half_dim = values.shape[-1] // 2
    rolled = jnp.concatenate((-values[..., half_dim:], values[..., :half_dim]), axis=-1)
    return values * cosine[:, None, :] + rolled * sine_table[:, None, :]

def forward(tok_in, prefix, g_attn, w_query, w_key, w_value, w_output, g_mlp, w_gate, w_up, w_down):

    def one_seq(packed):
        seq_in, prefix_len = packed
        length = seq_in.shape[0]
        nrm_one = normalize(seq_in)
        xn_one = low(nrm_one * g_attn)
        q_raw = low_back(jnp.dot(xn_one, w_query, precision=HIGH))
        k_raw = low_back(jnp.dot(xn_one, w_key, precision=HIGH))
        v_raw = low_back(jnp.dot(xn_one, w_value, precision=HIGH))
        cosine, sine_table = rotary(0, length, HD)
        q_heads = low(rotate(q_raw.reshape(length, H, HD), cosine, sine_table)).reshape(length, KVH, H // KVH, HD)
        k_heads = low(rotate(k_raw.reshape(length, KVH, HD), cosine, sine_table))
        v_heads = low(v_raw).reshape(length, KVH, HD)
        scores = low_back(jnp.einsum('tkgd,skd->kgts', q_heads, k_heads, precision=HIGH) * HD ** (-0.5))
        positions = lax.iota(jnp.int32, length)
        seen = (positions[None, :] <= positions[:, None]) | (positions[None, :] < prefix_len)
        scores = jnp.where(seen, scores, NEG)
        prob_low = low(jax.nn.softmax(scores, axis=-1))
        attn_o = jnp.einsum('kgts,skd->tkgd', prob_low, v_heads, precision=HIGH).reshape(length, H * HD)
        attn_o = low(low_back(attn_o))
        hid_res = seq_in + low_back(jnp.dot(attn_o, w_output, precision=HIGH))
        nrm_two = normalize(hid_res)
        xn_two = low(nrm_two * g_mlp)
        gate = low_back(jnp.dot(xn_two, w_gate, precision=HIGH))
        up_val = low_back(jnp.dot(xn_two, w_up, precision=HIGH))
        hidden = low(jax.nn.silu(gate) * up_val)
        return hid_res + jnp.dot(hidden, w_down, precision=HIGH)
    return lax.map(jax.checkpoint(one_seq), (tok_in, prefix))

def reference(tokens, prefix, g_attn, w_query, w_key, w_value, w_output, g_mlp, w_gate, w_up, w_down, cotangent):

    def wrapped(tok_in, gain_one, query_w, key_w, value_w, output_w, gain_two, gate_w, up_w, down_w):
        return forward(tok_in, prefix, gain_one, query_w, key_w, value_w, output_w, gain_two, gate_w, up_w, down_w)
    out_val, pull = jax.vjp(wrapped, tokens.astype(jnp.float32), g_attn.astype(jnp.float32), w_query.astype(jnp.float32), w_key.astype(jnp.float32), w_value.astype(jnp.float32), w_output.astype(jnp.float32), g_mlp.astype(jnp.float32), w_gate.astype(jnp.float32), w_up.astype(jnp.float32), w_down.astype(jnp.float32))
    grads = pull(cotangent.astype(jnp.float32))
    return (out_val.astype(jnp.bfloat16), grads[0].astype(jnp.bfloat16), grads[1], grads[2], grads[3], grads[4], grads[5], grads[6], grads[7], grads[8], grads[9])
```

```python
import jax
import jax.numpy as jnp
from jax import lax
from jax.sharding import PartitionSpec as P

FF = 8192
H = 8
KVH = 4
HD = 256
KEYBLK = 512


EPS = 1e-06
THETA = 1000042.0
NEG = -1e30


def mul_plain(first_op, second_op):
    return jnp.dot(first_op, second_op, preferred_element_type=jnp.float32)


def mul_right(first_op, second_op):
    return lax.dot_general(
        first_op, second_op, (((1,), (1,)), ((), ())), preferred_element_type=jnp.float32
    )


def mul_left(first_op, second_op):
    return lax.dot_general(
        first_op, second_op, (((0,), (0,)), ((), ())), preferred_element_type=jnp.float32
    )


def normalize(values):
    return values * lax.rsqrt(jnp.mean(values * values, axis=-1, keepdims=True) + EPS)


def norm_back(values, normed, grad_normed):
    factor = lax.rsqrt(jnp.mean(values * values, axis=-1, keepdims=True) + EPS)
    return factor * (grad_normed - normed * jnp.mean(grad_normed * normed, axis=-1, keepdims=True))


def rotary(first_pos, length, head_dim):
    half_dim = head_dim // 2
    frequency = 1.0 / THETA ** (lax.iota(jnp.float32, half_dim) * (2.0 / head_dim))
    angles = (first_pos + lax.iota(jnp.int32, length)).astype(jnp.float32)[:, None] * frequency[
        None, :
    ]
    cosine = jnp.concatenate((jnp.cos(angles), jnp.cos(angles)), axis=1)
    sine_table = jnp.concatenate((jnp.sin(angles), jnp.sin(angles)), axis=1)
    return (cosine, sine_table)


def rotate(values, cosine, sine_table):
    half_dim = values.shape[-1] // 2
    rolled = jnp.concatenate((-values[..., half_dim:], values[..., :half_dim]), axis=-1)
    return values * cosine[:, None, :] + rolled * sine_table[:, None, :]


def gathered_weights(
    tokens,
    prefix,
    g_attn,
    w_query,
    w_key,
    w_value,
    w_output,
    g_mlp,
    w_gate,
    w_up,
    w_down,
    cotangent,
):
    tok_rows = tokens.shape[1]
    key_span = lax.axis_size("ctx") * tok_rows
    first_pos = lax.axis_index("ctx") * tok_rows
    head_group = H // KVH
    query_width = H * HD
    key_width = KVH * HD
    score_scale = HD ** (-0.5)
    key_blocks = key_span // KEYBLK
    prefix_len = prefix[0]
    tok_in = tokens[0].astype(jnp.float32)
    nrm_one = normalize(tok_in)
    cosine, sine_table = rotary(first_pos, tok_rows, HD)
    query_pos = first_pos + lax.iota(jnp.int32, tok_rows)

    def visible(key_first, length):
        key_pos = key_first + lax.iota(jnp.int32, length)
        return (key_pos[None, :] <= query_pos[:, None]) | (key_pos[None, :] < prefix_len)

    gain_piece = lax.all_gather(g_attn, ("dp", "ctx"), axis=0, tiled=True)
    query_piece = lax.all_gather(w_query, ("dp", "ctx"), axis=0, tiled=True)
    key_piece = lax.all_gather(w_key, ("dp", "ctx"), axis=0, tiled=True)
    value_piece = lax.all_gather(w_value, ("dp", "ctx"), axis=0, tiled=True)
    length = gain_piece.shape[0]
    scaled = (nrm_one * gain_piece.astype(jnp.float32)).astype(jnp.bfloat16)
    q_raw = mul_plain(scaled, query_piece)
    k_raw = mul_plain(scaled, key_piece)
    v_raw = mul_plain(scaled, value_piece)
    xn_one = scaled
    query_low = rotate(q_raw.reshape(tok_rows, H, HD), cosine, sine_table).astype(jnp.bfloat16)
    query_low = query_low.reshape(tok_rows, KVH, head_group, HD)
    key_low = (
        rotate(k_raw.reshape(tok_rows, KVH, HD), cosine, sine_table)
        .astype(jnp.bfloat16)
        .reshape(tok_rows, key_width)
    )
    value_low = v_raw.astype(jnp.bfloat16)
    key_all, value_all = (
        lax.all_gather(key_low, "ctx", axis=0, tiled=True),
        lax.all_gather(value_low, "ctx", axis=0, tiled=True),
    )
    keys_heads = key_all.reshape(key_span, KVH, HD)
    values_heads = value_all.reshape(key_span, KVH, HD)
    scores = (
        jnp.einsum("tkgd,skd->kgts", query_low, keys_heads, preferred_element_type=jnp.float32)
        * score_scale
    )
    scores = jnp.where(visible(0, key_span), scores, NEG)
    row_max = jnp.max(scores, axis=-1, keepdims=True)
    log_total = row_max + jnp.log(jnp.sum(jnp.exp(scores - row_max), axis=-1, keepdims=True))
    prob_low = jnp.exp(scores - log_total).astype(jnp.bfloat16)
    attn_o = jnp.einsum(
        "kgts,skd->tkgd", prob_low, values_heads, preferred_element_type=jnp.float32
    )
    attn_o = attn_o.reshape(tok_rows, query_width).astype(jnp.bfloat16)
    attn_out = mul_plain(attn_o, lax.all_gather(w_output, ("dp", "ctx"), axis=0, tiled=True))
    hid_res = tok_in + attn_out
    nrm_two = normalize(hid_res)
    gain_piece = lax.all_gather(g_mlp, ("dp", "ctx"), axis=0, tiled=True)
    gate_piece = lax.all_gather(w_gate, ("dp", "ctx"), axis=0, tiled=True)
    up_piece = lax.all_gather(w_up, ("dp", "ctx"), axis=0, tiled=True)
    length = gain_piece.shape[0]
    scaled = (nrm_two * gain_piece.astype(jnp.float32)).astype(jnp.bfloat16)
    gate = mul_plain(scaled, gate_piece)
    up_val = mul_plain(scaled, up_piece)
    sigmoid_gate = jax.nn.sigmoid(gate)
    hidden = (gate * sigmoid_gate * up_val).astype(jnp.bfloat16)
    mlp_out = mul_plain(hidden, lax.all_gather(w_down, ("dp", "ctx"), axis=0, tiled=True))
    result = (hid_res + mlp_out).astype(jnp.bfloat16)[None]
    grad_y = cotangent[0]
    grad_hidden = mul_right(grad_y, lax.all_gather(w_down, ("dp", "ctx"), axis=0, tiled=True))
    grad_gate_low = (
        grad_hidden * up_val * sigmoid_gate * (1.0 + gate * (1.0 - sigmoid_gate))
    ).astype(jnp.bfloat16)
    grad_up_low = (grad_hidden * gate * sigmoid_gate).astype(jnp.bfloat16)
    gain_piece = lax.all_gather(g_mlp, ("dp", "ctx"), axis=0, tiled=True)
    gate_piece = lax.all_gather(w_gate, ("dp", "ctx"), axis=0, tiled=True)
    up_piece = lax.all_gather(w_up, ("dp", "ctx"), axis=0, tiled=True)
    summed = mul_right(grad_gate_low, gate_piece) + mul_right(grad_up_low, up_piece)
    stacked = jnp.stack((summed * gain_piece.astype(jnp.float32), summed))
    mlp_pair = stacked
    gain_two_grad = jnp.sum(mlp_pair[1] * nrm_two, axis=0)
    d_res = grad_y.astype(jnp.float32) + norm_back(hid_res, nrm_two, mlp_pair[0])
    gate_up_low = jnp.concatenate((grad_gate_low, grad_up_low), axis=1)
    gate_up_grad = lax.psum_scatter(
        mul_left(scaled, gate_up_low), ("dp", "ctx"), scatter_dimension=0, tiled=True
    )
    down_grad = lax.psum_scatter(
        mul_left(hidden, grad_y), ("dp", "ctx"), scatter_dimension=0, tiled=True
    )
    d_res_low = d_res.astype(jnp.bfloat16)
    grad_attn = mul_right(d_res_low, lax.all_gather(w_output, ("dp", "ctx"), axis=0, tiled=True))
    grad_attn_low = grad_attn.astype(jnp.bfloat16).reshape(tok_rows, KVH, head_group, HD)

    def block_parts(block_id):
        key_first = block_id * KEYBLK
        key_block = lax.dynamic_slice_in_dim(keys_heads, key_first, KEYBLK, 0)
        value_block = lax.dynamic_slice_in_dim(values_heads, key_first, KEYBLK, 0)
        block_scores = (
            jnp.einsum("tkgd,skd->kgts", query_low, key_block, preferred_element_type=jnp.float32)
            * score_scale
        )
        block_scores = jnp.where(visible(key_first, KEYBLK), block_scores, NEG)
        prob_full = jnp.exp(block_scores - log_total)
        grad_prob = jnp.einsum(
            "tkgd,skd->kgts", grad_attn_low, value_block, preferred_element_type=jnp.float32
        )
        return (key_block, prob_full, grad_prob)

    def delta_step(summed, block_id):
        unused_keys, prob_full, grad_prob = block_parts(block_id)
        return (summed + jnp.sum(prob_full * grad_prob, axis=-1, keepdims=True), None)

    row_delta, unused_out = lax.scan(
        delta_step, jnp.zeros(log_total.shape, jnp.float32), lax.iota(jnp.int32, key_blocks)
    )

    def grad_step(grad_query, block_id):
        key_block, prob_full, grad_prob = block_parts(block_id)
        grad_score = (prob_full * (grad_prob - row_delta)).astype(jnp.bfloat16)
        grad_query = (
            grad_query
            + jnp.einsum(
                "kgts,skd->tkgd", grad_score, key_block, preferred_element_type=jnp.float32
            )
            * score_scale
        )
        grad_key_block = (
            jnp.einsum("kgts,tkgd->skd", grad_score, query_low, preferred_element_type=jnp.float32)
            * score_scale
        )
        grad_value_block = jnp.einsum(
            "kgts,tkgd->skd",
            prob_full.astype(jnp.bfloat16),
            grad_attn_low,
            preferred_element_type=jnp.float32,
        )
        return (
            grad_query,
            (
                grad_key_block.reshape(KEYBLK, key_width),
                grad_value_block.reshape(KEYBLK, key_width),
            ),
        )

    grad_query, block_grads = lax.scan(
        grad_step,
        jnp.zeros((tok_rows, KVH, head_group, HD), jnp.float32),
        lax.iota(jnp.int32, key_blocks),
    )
    keys_grad_all = block_grads[0].reshape(key_span, key_width)
    values_grad_all = block_grads[1].reshape(key_span, key_width)
    key_grad_own, value_grad_own = (
        lax.psum_scatter(
            keys_grad_all.astype(jnp.bfloat16), "ctx", scatter_dimension=0, tiled=True
        ).astype(jnp.float32),
        lax.psum_scatter(
            values_grad_all.astype(jnp.bfloat16), "ctx", scatter_dimension=0, tiled=True
        ).astype(jnp.float32),
    )
    query_grad_low = rotate(grad_query.reshape(tok_rows, H, HD), cosine, -sine_table).astype(
        jnp.bfloat16
    )
    query_grad_low = query_grad_low.reshape(tok_rows, query_width)
    key_grad_low = rotate(key_grad_own.reshape(tok_rows, KVH, HD), cosine, -sine_table).astype(
        jnp.bfloat16
    )
    key_grad_low = key_grad_low.reshape(tok_rows, key_width)
    value_grad_low = value_grad_own.astype(jnp.bfloat16)
    gain_piece = lax.all_gather(g_attn, ("dp", "ctx"), axis=0, tiled=True)
    query_piece = lax.all_gather(w_query, ("dp", "ctx"), axis=0, tiled=True)
    key_piece = lax.all_gather(w_key, ("dp", "ctx"), axis=0, tiled=True)
    value_piece = lax.all_gather(w_value, ("dp", "ctx"), axis=0, tiled=True)
    summed = (
        mul_right(query_grad_low, query_piece)
        + mul_right(key_grad_low, key_piece)
        + mul_right(value_grad_low, value_piece)
    )
    stacked = jnp.stack((summed * gain_piece.astype(jnp.float32), summed))
    gain_one_grad = jnp.sum(stacked[1] * nrm_one, axis=0)
    input_grad = (d_res + norm_back(tok_in, nrm_one, stacked[0])).astype(jnp.bfloat16)[None]
    qkv_grad_low = jnp.concatenate((query_grad_low, key_grad_low, value_grad_low), axis=1)
    first_part = mul_left(xn_one, qkv_grad_low)
    second_part = mul_left(attn_o, d_res_low)
    attn_grad = lax.psum_scatter(
        jnp.concatenate((first_part, second_part), axis=1),
        ("dp", "ctx"),
        scatter_dimension=0,
        tiled=True,
    )
    gain_grads = (
        lax.psum_scatter(gain_one_grad, ("dp", "ctx"), scatter_dimension=0, tiled=True),
        lax.psum_scatter(gain_two_grad, ("dp", "ctx"), scatter_dimension=0, tiled=True),
    )
    return (
        result,
        input_grad,
        gain_grads[0],
        attn_grad[:, :query_width],
        attn_grad[:, query_width : query_width + key_width],
        attn_grad[:, query_width + key_width : query_width + 2 * key_width],
        attn_grad[:, query_width + 2 * key_width :],
        gain_grads[1],
        gate_up_grad[:, :FF],
        gate_up_grad[:, FF:],
        down_grad,
    )


def scatter_ctx(values):
    return lax.psum_scatter(values, "ctx", scatter_dimension=0, tiled=True)


def gather_ctx(values):
    return lax.all_gather(values, "ctx", axis=0, tiled=True)


def swap_ctx(values):
    return lax.all_to_all(values, "ctx", split_axis=0, concat_axis=0, tiled=True)


def head_split(
    tokens,
    prefix,
    g_attn,
    w_query,
    w_key,
    w_value,
    w_output,
    g_mlp,
    w_gate,
    w_up,
    w_down,
    cotangent,
):
    bf16, f32 = jnp.bfloat16, jnp.float32
    groups, pieces = lax.axis_size("ctx"), lax.axis_size("dp")
    tok_rows, width = tokens.shape[1:]
    span = groups * tok_rows
    shard = w_query.shape[0]
    share = w_down.shape[0]
    per_key = H // KVH

    tok_in = tokens[0].astype(f32)
    gain_one, gain_two = g_attn.astype(f32)[:, None], g_mlp.astype(f32)[:, None]

    q_cols = (gain_one * w_query).astype(bf16).reshape(shard, H, HD)
    k_cols = jnp.repeat((gain_one * w_key).astype(bf16).reshape(shard, KVH, HD), per_key, axis=1)
    v_cols = jnp.repeat((gain_one * w_value).astype(bf16).reshape(shard, KVH, HD), per_key, axis=1)
    qkv_cols = jnp.concatenate((q_cols, k_cols, v_cols), axis=2).transpose(1, 0, 2)
    qkv_w = lax.all_gather(
        swap_ctx(qkv_cols).reshape(groups * shard, 3 * HD), "dp", axis=0, tiled=True
    )
    tok_all = gather_ctx(tokens[0])
    xn_one = normalize(tok_all.astype(f32)).astype(bf16)
    qkv = mul_plain(xn_one, qkv_w)

    def gated(weight):
        scaled = (gain_two * weight).astype(bf16).reshape(shard, pieces, groups, share)
        return scaled.transpose(2, 0, 1, 3).reshape(groups, shard, pieces * share)

    gate_up_w = lax.all_gather(
        swap_ctx(jnp.concatenate((gated(w_gate), gated(w_up)), axis=2)).reshape(
            groups * shard, 2 * pieces * share
        ),
        "dp",
        axis=0,
        tiled=True,
    )
    down_w = lax.all_gather(w_down, "dp", axis=0, tiled=True)
    output_w = lax.all_gather(w_output, ("dp", "ctx"), axis=0, tiled=True)

    cosine, sine = rotary(0, span, HD)

    def turn(values, sine_table):
        half = HD // 2
        rolled = jnp.concatenate((-values[:, half:], values[:, :half]), axis=-1)
        return values * cosine + rolled * sine_table

    query = turn(qkv[:, :HD], sine).astype(bf16)
    key = turn(qkv[:, HD : 2 * HD], sine).astype(bf16)
    value = qkv[:, 2 * HD :].astype(bf16)
    scores = mul_right(query, key) * HD ** (-0.5)
    pos = lax.iota(jnp.int32, span)
    seen = (pos[None, :] <= pos[:, None]) | (pos[None, :] < prefix[0])
    scores = jnp.where(seen, scores, NEG)
    prob = jax.nn.softmax(scores, axis=-1)
    prob_low = prob.astype(bf16)
    head_o = mul_plain(prob_low, value)

    attn_o = swap_ctx(head_o.astype(bf16).reshape(groups, tok_rows, HD))
    attn_o = attn_o.transpose(1, 0, 2).reshape(tok_rows, H * HD)
    hid_res = tok_in + mul_plain(attn_o, output_w)
    nrm_two = normalize(hid_res)
    xn_two = gather_ctx(nrm_two.astype(bf16))
    gate_up = mul_plain(xn_two, gate_up_w)
    gate, up_val = gate_up[:, : pieces * share], gate_up[:, pieces * share :]
    sigmoid_gate = jax.nn.sigmoid(gate)
    hidden = (gate * sigmoid_gate * up_val).astype(bf16)
    result = hid_res + scatter_ctx(mul_plain(hidden, down_w).astype(bf16)).astype(f32)
    result = result.astype(bf16)[None]

    dy_all = gather_ctx(cotangent[0])
    d_hidden = mul_right(dy_all, down_w)
    d_gate = d_hidden * up_val * sigmoid_gate * (1.0 + gate * (1.0 - sigmoid_gate))
    d_up = d_hidden * gate * sigmoid_gate
    d_gate_up = jnp.concatenate((d_gate.astype(bf16), d_up.astype(bf16)), axis=1)
    dn_two = scatter_ctx(mul_right(d_gate_up, gate_up_w).astype(bf16)).astype(f32)
    d_res = cotangent[0].astype(f32) + norm_back(hid_res, nrm_two, dn_two)
    d_res_low = d_res.astype(bf16)

    def scatter_dp(values):
        return lax.psum_scatter(values.astype(bf16), "dp", scatter_dimension=0, tiled=True)

    down_grad = scatter_dp(mul_left(hidden, dy_all)).astype(f32)
    gate_up_sum = swap_ctx(
        scatter_dp(mul_left(xn_two, d_gate_up)).reshape(groups, shard, 2 * pieces * share)
    ).astype(f32)

    def ungated(summed):
        return summed.reshape(groups, shard, pieces, share).transpose(1, 2, 0, 3).reshape(shard, FF)

    gate_sum = ungated(gate_up_sum[:, :, : pieces * share])
    up_sum = ungated(gate_up_sum[:, :, pieces * share :])
    gain_two_grad = jnp.sum(w_gate * gate_sum + w_up * up_sum, axis=1)

    d_attn = mul_right(d_res_low, output_w).astype(bf16)
    d_head = swap_ctx(d_attn.reshape(tok_rows, groups, HD).transpose(1, 0, 2)).reshape(span, HD)
    output_grad = lax.psum_scatter(
        mul_left(attn_o, d_res_low).astype(bf16), ("dp", "ctx"), scatter_dimension=0, tiled=True
    ).astype(f32)

    d_prob = mul_right(d_head, value)
    row_delta = jnp.sum(prob * d_prob, axis=-1, keepdims=True)
    d_score = (prob * (d_prob - row_delta)).astype(bf16)
    d_query = turn(mul_plain(d_score, key) * HD ** (-0.5), -sine)
    d_key = turn(mul_left(d_score, query) * HD ** (-0.5), -sine)
    d_value = mul_left(prob_low, d_head)
    d_qkv = jnp.concatenate((d_query, d_key, d_value), axis=1).astype(bf16)
    dn_one = scatter_ctx(mul_right(d_qkv, qkv_w).astype(bf16)).astype(f32)
    input_grad = d_res + norm_back(tok_in, normalize(tok_in), dn_one)
    input_grad = input_grad.astype(bf16)[None]

    qkv_sum = swap_ctx(scatter_dp(mul_left(xn_one, d_qkv)).reshape(groups, shard, 3 * HD))
    qkv_sum = qkv_sum.astype(f32).transpose(1, 0, 2)
    q_sum = qkv_sum[:, :, :HD].reshape(shard, H * HD)

    def per_group(summed):
        return jnp.sum(summed.reshape(shard, KVH, per_key, HD), axis=2).reshape(shard, KVH * HD)

    k_sum = per_group(qkv_sum[:, :, HD : 2 * HD])
    v_sum = per_group(qkv_sum[:, :, 2 * HD :])
    gain_one_grad = (
        jnp.sum(w_query * q_sum, axis=1)
        + jnp.sum(w_key * k_sum, axis=1)
        + jnp.sum(w_value * v_sum, axis=1)
    )
    return (
        result,
        input_grad,
        gain_one_grad,
        gain_one * q_sum,
        gain_one * k_sum,
        gain_one * v_sum,
        output_grad,
        gain_two_grad,
        gain_two * gate_sum,
        gain_two * up_sum,
        down_grad,
    )


def solution(mesh):
    one_head_each = mesh.shape["ctx"] == H
    rows, whole = P(("dp", "ctx")), P(("dp", "ctx"), None)
    acts = P("dp", "ctx", None)
    in_specs = (acts, P("dp"), rows, whole, whole, whole, whole, rows, whole, whole, whole, acts)
    out_specs = (acts, acts, rows, whole, whole, whole, whole, rows, whole, whole, whole)
    return jax.shard_map(
        head_split if one_head_each else gathered_weights,
        mesh=mesh,
        in_specs=in_specs,
        out_specs=out_specs,
        check_vma=False,
    )
```

```python
import jax
import jax.numpy as jnp
from jax import lax
from jax.sharding import Mesh
from jax.sharding import PartitionSpec as P

FF = 8192
H = 8
KVH = 4
HD = 256
KEYBLK = 512


EPS = 1e-06
THETA = 1000042.0
NEG = -1e30


def mul_plain(first_op, second_op):
    return jnp.dot(first_op, second_op, preferred_element_type=jnp.float32)


def mul_right(first_op, second_op):
    return lax.dot_general(
        first_op, second_op, (((1,), (1,)), ((), ())), preferred_element_type=jnp.float32
    )


def mul_left(first_op, second_op):
    return lax.dot_general(
        first_op, second_op, (((0,), (0,)), ((), ())), preferred_element_type=jnp.float32
    )


def normalize(values):
    return values * lax.rsqrt(jnp.mean(values * values, axis=-1, keepdims=True) + EPS)


def norm_back(values, normed, grad_normed):
    factor = lax.rsqrt(jnp.mean(values * values, axis=-1, keepdims=True) + EPS)
    return factor * (grad_normed - normed * jnp.mean(grad_normed * normed, axis=-1, keepdims=True))


def rotary(first_pos, length, head_dim):
    half_dim = head_dim // 2
    frequency = 1.0 / THETA ** (lax.iota(jnp.float32, half_dim) * (2.0 / head_dim))
    angles = (first_pos + lax.iota(jnp.int32, length)).astype(jnp.float32)[:, None] * frequency[
        None, :
    ]
    cosine = jnp.concatenate((jnp.cos(angles), jnp.cos(angles)), axis=1)
    sine_table = jnp.concatenate((jnp.sin(angles), jnp.sin(angles)), axis=1)
    return (cosine, sine_table)


def rotate(values, cosine, sine_table):
    half_dim = values.shape[-1] // 2
    rolled = jnp.concatenate((-values[..., half_dim:], values[..., :half_dim]), axis=-1)
    return values * cosine[:, None, :] + rolled * sine_table[:, None, :]


def gathered_weights(
    tokens,
    prefix,
    g_attn,
    w_query,
    w_key,
    w_value,
    w_output,
    g_mlp,
    w_gate,
    w_up,
    w_down,
    cotangent,
):
    tok_rows = tokens.shape[1]
    key_span = lax.axis_size("ctx") * tok_rows
    first_pos = lax.axis_index("ctx") * tok_rows
    head_group = H // KVH
    query_width = H * HD
    key_width = KVH * HD
    score_scale = HD ** (-0.5)
    key_blocks = key_span // KEYBLK
    prefix_len = prefix[0]
    tok_in = tokens[0].astype(jnp.float32)
    nrm_one = normalize(tok_in)
    cosine, sine_table = rotary(first_pos, tok_rows, HD)
    query_pos = first_pos + lax.iota(jnp.int32, tok_rows)

    def visible(key_first, length):
        key_pos = key_first + lax.iota(jnp.int32, length)
        return (key_pos[None, :] <= query_pos[:, None]) | (key_pos[None, :] < prefix_len)

    gain_piece = lax.all_gather(g_attn, ("dp", "ctx"), axis=0, tiled=True)
    query_piece = lax.all_gather(w_query, ("dp", "ctx"), axis=0, tiled=True)
    key_piece = lax.all_gather(w_key, ("dp", "ctx"), axis=0, tiled=True)
    value_piece = lax.all_gather(w_value, ("dp", "ctx"), axis=0, tiled=True)
    length = gain_piece.shape[0]
    scaled = (nrm_one * gain_piece.astype(jnp.float32)).astype(jnp.bfloat16)
    q_raw = mul_plain(scaled, query_piece)
    k_raw = mul_plain(scaled, key_piece)
    v_raw = mul_plain(scaled, value_piece)
    xn_one = scaled
    query_low = rotate(q_raw.reshape(tok_rows, H, HD), cosine, sine_table).astype(jnp.bfloat16)
    query_low = query_low.reshape(tok_rows, KVH, head_group, HD)
    key_low = (
        rotate(k_raw.reshape(tok_rows, KVH, HD), cosine, sine_table)
        .astype(jnp.bfloat16)
        .reshape(tok_rows, key_width)
    )
    value_low = v_raw.astype(jnp.bfloat16)
    key_all, value_all = (
        lax.all_gather(key_low, "ctx", axis=0, tiled=True),
        lax.all_gather(value_low, "ctx", axis=0, tiled=True),
    )
    keys_heads = key_all.reshape(key_span, KVH, HD)
    values_heads = value_all.reshape(key_span, KVH, HD)
    scores = (
        jnp.einsum("tkgd,skd->kgts", query_low, keys_heads, preferred_element_type=jnp.float32)
        * score_scale
    )
    scores = jnp.where(visible(0, key_span), scores, NEG)
    row_max = jnp.max(scores, axis=-1, keepdims=True)
    log_total = row_max + jnp.log(jnp.sum(jnp.exp(scores - row_max), axis=-1, keepdims=True))
    prob_low = jnp.exp(scores - log_total).astype(jnp.bfloat16)
    attn_o = jnp.einsum(
        "kgts,skd->tkgd", prob_low, values_heads, preferred_element_type=jnp.float32
    )
    attn_o = attn_o.reshape(tok_rows, query_width).astype(jnp.bfloat16)
    attn_out = mul_plain(attn_o, lax.all_gather(w_output, ("dp", "ctx"), axis=0, tiled=True))
    hid_res = tok_in + attn_out
    nrm_two = normalize(hid_res)
    gain_piece = lax.all_gather(g_mlp, ("dp", "ctx"), axis=0, tiled=True)
    gate_piece = lax.all_gather(w_gate, ("dp", "ctx"), axis=0, tiled=True)
    up_piece = lax.all_gather(w_up, ("dp", "ctx"), axis=0, tiled=True)
    length = gain_piece.shape[0]
    scaled = (nrm_two * gain_piece.astype(jnp.float32)).astype(jnp.bfloat16)
    gate = mul_plain(scaled, gate_piece)
    up_val = mul_plain(scaled, up_piece)
    sigmoid_gate = jax.nn.sigmoid(gate)
    hidden = (gate * sigmoid_gate * up_val).astype(jnp.bfloat16)
    mlp_out = mul_plain(hidden, lax.all_gather(w_down, ("dp", "ctx"), axis=0, tiled=True))
    result = (hid_res + mlp_out).astype(jnp.bfloat16)[None]
    grad_y = cotangent[0]
    grad_hidden = mul_right(grad_y, lax.all_gather(w_down, ("dp", "ctx"), axis=0, tiled=True))
    grad_gate_low = (
        grad_hidden * up_val * sigmoid_gate * (1.0 + gate * (1.0 - sigmoid_gate))
    ).astype(jnp.bfloat16)
    grad_up_low = (grad_hidden * gate * sigmoid_gate).astype(jnp.bfloat16)
    gain_piece = lax.all_gather(g_mlp, ("dp", "ctx"), axis=0, tiled=True)
    gate_piece = lax.all_gather(w_gate, ("dp", "ctx"), axis=0, tiled=True)
    up_piece = lax.all_gather(w_up, ("dp", "ctx"), axis=0, tiled=True)
    summed = mul_right(grad_gate_low, gate_piece) + mul_right(grad_up_low, up_piece)
    stacked = jnp.stack((summed * gain_piece.astype(jnp.float32), summed))
    mlp_pair = stacked
    gain_two_grad = jnp.sum(mlp_pair[1] * nrm_two, axis=0)
    d_res = grad_y.astype(jnp.float32) + norm_back(hid_res, nrm_two, mlp_pair[0])
    gate_up_low = jnp.concatenate((grad_gate_low, grad_up_low), axis=1)
    gate_up_grad = lax.psum_scatter(
        mul_left(scaled, gate_up_low), ("dp", "ctx"), scatter_dimension=0, tiled=True
    )
    down_grad = lax.psum_scatter(
        mul_left(hidden, grad_y), ("dp", "ctx"), scatter_dimension=0, tiled=True
    )
    d_res_low = d_res.astype(jnp.bfloat16)
    grad_attn = mul_right(d_res_low, lax.all_gather(w_output, ("dp", "ctx"), axis=0, tiled=True))
    grad_attn_low = grad_attn.astype(jnp.bfloat16).reshape(tok_rows, KVH, head_group, HD)

    def block_parts(block_id):
        key_first = block_id * KEYBLK
        key_block = lax.dynamic_slice_in_dim(keys_heads, key_first, KEYBLK, 0)
        value_block = lax.dynamic_slice_in_dim(values_heads, key_first, KEYBLK, 0)
        block_scores = (
            jnp.einsum("tkgd,skd->kgts", query_low, key_block, preferred_element_type=jnp.float32)
            * score_scale
        )
        block_scores = jnp.where(visible(key_first, KEYBLK), block_scores, NEG)
        prob_full = jnp.exp(block_scores - log_total)
        grad_prob = jnp.einsum(
            "tkgd,skd->kgts", grad_attn_low, value_block, preferred_element_type=jnp.float32
        )
        return (key_block, prob_full, grad_prob)

    def delta_step(summed, block_id):
        unused_keys, prob_full, grad_prob = block_parts(block_id)
        return (summed + jnp.sum(prob_full * grad_prob, axis=-1, keepdims=True), None)

    row_delta, unused_out = lax.scan(
        delta_step, jnp.zeros(log_total.shape, jnp.float32), lax.iota(jnp.int32, key_blocks)
    )

    def grad_step(grad_query, block_id):
        key_block, prob_full, grad_prob = block_parts(block_id)
        grad_score = (prob_full * (grad_prob - row_delta)).astype(jnp.bfloat16)
        grad_query = (
            grad_query
            + jnp.einsum(
                "kgts,skd->tkgd", grad_score, key_block, preferred_element_type=jnp.float32
            )
            * score_scale
        )
        grad_key_block = (
            jnp.einsum("kgts,tkgd->skd", grad_score, query_low, preferred_element_type=jnp.float32)
            * score_scale
        )
        grad_value_block = jnp.einsum(
            "kgts,tkgd->skd",
            prob_full.astype(jnp.bfloat16),
            grad_attn_low,
            preferred_element_type=jnp.float32,
        )
        return (
            grad_query,
            (
                grad_key_block.reshape(KEYBLK, key_width),
                grad_value_block.reshape(KEYBLK, key_width),
            ),
        )

    grad_query, block_grads = lax.scan(
        grad_step,
        jnp.zeros((tok_rows, KVH, head_group, HD), jnp.float32),
        lax.iota(jnp.int32, key_blocks),
    )
    keys_grad_all = block_grads[0].reshape(key_span, key_width)
    values_grad_all = block_grads[1].reshape(key_span, key_width)
    key_grad_own, value_grad_own = (
        lax.psum_scatter(
            keys_grad_all.astype(jnp.bfloat16), "ctx", scatter_dimension=0, tiled=True
        ).astype(jnp.float32),
        lax.psum_scatter(
            values_grad_all.astype(jnp.bfloat16), "ctx", scatter_dimension=0, tiled=True
        ).astype(jnp.float32),
    )
    query_grad_low = rotate(grad_query.reshape(tok_rows, H, HD), cosine, -sine_table).astype(
        jnp.bfloat16
    )
    query_grad_low = query_grad_low.reshape(tok_rows, query_width)
    key_grad_low = rotate(key_grad_own.reshape(tok_rows, KVH, HD), cosine, -sine_table).astype(
        jnp.bfloat16
    )
    key_grad_low = key_grad_low.reshape(tok_rows, key_width)
    value_grad_low = value_grad_own.astype(jnp.bfloat16)
    gain_piece = lax.all_gather(g_attn, ("dp", "ctx"), axis=0, tiled=True)
    query_piece = lax.all_gather(w_query, ("dp", "ctx"), axis=0, tiled=True)
    key_piece = lax.all_gather(w_key, ("dp", "ctx"), axis=0, tiled=True)
    value_piece = lax.all_gather(w_value, ("dp", "ctx"), axis=0, tiled=True)
    summed = (
        mul_right(query_grad_low, query_piece)
        + mul_right(key_grad_low, key_piece)
        + mul_right(value_grad_low, value_piece)
    )
    stacked = jnp.stack((summed * gain_piece.astype(jnp.float32), summed))
    gain_one_grad = jnp.sum(stacked[1] * nrm_one, axis=0)
    input_grad = (d_res + norm_back(tok_in, nrm_one, stacked[0])).astype(jnp.bfloat16)[None]
    qkv_grad_low = jnp.concatenate((query_grad_low, key_grad_low, value_grad_low), axis=1)
    first_part = mul_left(xn_one, qkv_grad_low)
    second_part = mul_left(attn_o, d_res_low)
    attn_grad = lax.psum_scatter(
        jnp.concatenate((first_part, second_part), axis=1),
        ("dp", "ctx"),
        scatter_dimension=0,
        tiled=True,
    )
    gain_grads = (
        lax.psum_scatter(gain_one_grad, ("dp", "ctx"), scatter_dimension=0, tiled=True),
        lax.psum_scatter(gain_two_grad, ("dp", "ctx"), scatter_dimension=0, tiled=True),
    )
    return (
        result,
        input_grad,
        gain_grads[0],
        attn_grad[:, :query_width],
        attn_grad[:, query_width : query_width + key_width],
        attn_grad[:, query_width + key_width : query_width + 2 * key_width],
        attn_grad[:, query_width + 2 * key_width :],
        gain_grads[1],
        gate_up_grad[:, :FF],
        gate_up_grad[:, FF:],
        down_grad,
    )


BF16, F32 = jnp.bfloat16, jnp.float32
CTX = ("half", "low", "core")
TEAM = ("x", "low", "core")
join = lax.optimization_barrier


def put(buffer, block, index):
    return lax.dynamic_update_slice(buffer, block[None], (index,) + (0,) * block.ndim)


def take(values, index):
    return lax.dynamic_index_in_dim(values, index, 0, keepdims=False)


def after(values, *others):
    return join((values,) + others)[0]


def flip(values, axis, bits=1):
    return lax.ppermute(values, axis, [(i, i ^ bits) for i in range(lax.axis_size(axis))])


def send_dp(own):
    return [own] + [flip(own, ("y", "x"), bits) for bits in range(1, 4)]


def order_dp(blocks):
    d = lax.axis_index(("y", "x"))
    buffer = jnp.zeros((4,) + blocks[0].shape, blocks[0].dtype)
    for bits, block in enumerate(blocks):
        buffer = put(buffer, block, d ^ bits)
    return buffer


def send_parts_dp(parts):
    d = lax.axis_index(("y", "x"))
    away = [flip(take(parts, d ^ bits).astype(BF16), ("y", "x"), bits) for bits in range(1, 4)]
    return [take(parts, d)] + away


def add_parts(parts):
    total = parts[0]
    for part in parts[1:]:
        total = total + part.astype(F32)
    return total


def turn_chips(values, step):
    pairs = [(c, (c + 2 * step) % 8) for c in range(8)]
    return lax.ppermute(values, CTX, pairs)


def send_column(rows):
    return [rows] + [turn_chips(rows, step) for step in range(1, 4)]


def order_column(blocks):
    chip = lax.axis_index(("half", "low"))
    column = jnp.zeros((4,) + blocks[0].shape, blocks[0].dtype)
    for step, block in enumerate(blocks):
        column = put(column, block, (chip - step) % 4)
    return column


def order_cores(mine, other):
    core = lax.axis_index("core")
    low, high = jnp.where(core == 0, mine, other), jnp.where(core == 0, other, mine)
    return jnp.stack((low, high), axis=-3)


def order_teams(near, far, near_y, far_y):
    y, half = lax.axis_index("y"), lax.axis_index("half")
    buffer = jnp.zeros((4,) + near.shape, near.dtype)
    for block, bits in ((near, 0), (far, 1), (near_y, 2), (far_y, 3)):
        buffer = put(buffer, block, (2 * y + half) ^ bits)
    return buffer.reshape((2, 2) + near.shape)


def swap(values, axes):
    return lax.all_to_all(values, axes, split_axis=0, concat_axis=0, tiled=True)


def gather(values, axes):
    return lax.all_gather(values, axes, axis=0, tiled=True)


def scatter(values, axes):
    return lax.psum_scatter(values, axes, scatter_dimension=0, tiled=True).astype(F32)


def other_y(parts):
    return flip(take(parts, 1 - lax.axis_index("y")).astype(BF16), "y")


def add_y(parts, got):
    return take(parts, lax.axis_index("y")) + got.astype(F32)


def other_half(parts):
    return flip(take(parts, 1 - lax.axis_index("half")).astype(BF16), "half")


def add_half(parts, got):
    return take(parts, lax.axis_index("half")) + got.astype(F32)


def head_split(
    tokens,
    prefix,
    g_attn,
    w_query,
    w_key,
    w_value,
    w_output,
    g_mlp,
    w_gate,
    w_up,
    w_down,
    cotangent,
):
    groups = 8
    tok_rows, width = tokens.shape[1:]
    span = groups * tok_rows
    shard = w_query.shape[0]
    share = w_down.shape[0]
    slice_ff = 4 * share
    per_key = H // KVH
    scale = HD ** (-0.5)

    tok_in = tokens[0].astype(F32)
    gain_one, gain_two = g_attn.astype(F32)[:, None], g_mlp.astype(F32)[:, None]

    q_cols = (gain_one * w_query).astype(BF16).reshape(shard, H, HD)
    k_cols = jnp.repeat((gain_one * w_key).astype(BF16).reshape(shard, KVH, HD), per_key, axis=1)
    v_cols = jnp.repeat((gain_one * w_value).astype(BF16).reshape(shard, KVH, HD), per_key, axis=1)
    qkv_cols = jnp.concatenate((q_cols, k_cols, v_cols), axis=2).transpose(1, 0, 2)

    def gated(weight):
        scaled = (gain_two * weight).astype(BF16).reshape(shard, 4, groups, share)
        return scaled.transpose(2, 0, 1, 3).reshape(groups, shard, slice_ff)

    gate_cols, up_cols = gated(w_gate), gated(w_up)
    cosine, sine = rotary(0, span, HD)

    def turn(values, sine_table):
        half = HD // 2
        rolled = jnp.concatenate((-values[:, half:], values[:, :half]), axis=-1)
        return values * cosine + rolled * sine_table

    down_blocks = send_dp(w_down)
    tok_all = gather(tokens[0], CTX)
    qkv_rows = swap(qkv_cols, CTX).reshape(groups * shard, 3 * HD)
    qkv_rows, out_own, gate_cols, up_cols = join((qkv_rows, w_output, gate_cols, up_cols))
    qkv_blocks = send_dp(qkv_rows)
    out_blocks = send_column(out_own)
    qkv_w = order_dp(qkv_blocks).reshape(width, 3 * HD)
    out_rows = order_column(out_blocks)
    down_w = order_dp(down_blocks).reshape(slice_ff, width)
    tok_all, qkv_w, down_w, gate_cols, cosine, sine = join(
        (tok_all, qkv_w, down_w, gate_cols, cosine, sine)
    )
    out_mine = order_dp(send_dp(after(out_rows, qkv_w)))
    gate_rows = swap(gate_cols, CTX).reshape(groups * shard, slice_ff)
    xn_one = normalize(tok_all.astype(F32)).astype(BF16)
    qkv = mul_plain(xn_one, qkv_w)
    query = turn(qkv[:, :HD], sine).astype(BF16)
    key = turn(qkv[:, HD : 2 * HD], sine).astype(BF16)
    value = qkv[:, 2 * HD :].astype(BF16)
    query, key, value, gate_rows, up_cols, out_mine = join(
        (query, key, value, gate_rows, up_cols, out_mine)
    )
    gate_blocks = send_dp(gate_rows)
    up_rows = swap(up_cols, CTX).reshape(groups * shard, slice_ff)
    scores = mul_right(query, key) * scale
    pos = lax.iota(jnp.int32, span)
    seen = (pos[None, :] <= pos[:, None]) | (pos[None, :] < prefix[0])
    scores = jnp.where(seen, scores, NEG)
    prob = jax.nn.softmax(scores, axis=-1)
    prob_low = prob.astype(BF16)
    head_o = mul_plain(prob_low, value).astype(BF16)
    head_o, up_rows = join((head_o, up_rows))
    attn_o = swap(head_o.reshape(groups, tok_rows, HD), CTX)
    up_blocks = send_dp(up_rows)
    output_w = order_cores(out_mine, flip(out_mine, "core")).reshape(H * HD, width)
    attn_o, output_w, gate_blocks = join((attn_o, output_w, gate_blocks))
    attn_o = attn_o.transpose(1, 0, 2).reshape(tok_rows, H * HD)
    hid_res = tok_in + mul_plain(attn_o, output_w)
    nrm_two = normalize(hid_res)
    xn_two = gather(nrm_two.astype(BF16), CTX)
    gate_w = order_dp(gate_blocks).reshape(width, slice_ff)
    up_w = order_dp(up_blocks).reshape(width, slice_ff)
    xn_two, gate_w, up_w, dy_own = join((xn_two, gate_w, up_w, cotangent[0]))
    dy_all = gather(dy_own, CTX)
    gate, up_val = mul_plain(xn_two, gate_w), mul_plain(xn_two, up_w)
    sigmoid_gate = jax.nn.sigmoid(gate)
    hidden = (gate * sigmoid_gate * up_val).astype(BF16)
    mlp_part = mul_plain(hidden, down_w).astype(BF16)
    dy_all, mlp_part, gate, up_val = join((dy_all, mlp_part, gate, up_val))
    cut = width // 2
    mlp_low = scatter(mlp_part[:, :cut], CTX)
    sigmoid_gate = jax.nn.sigmoid(gate)
    d_hidden = mul_right(dy_all, down_w)
    d_gate = d_hidden * up_val * sigmoid_gate * (1.0 + gate * (1.0 - sigmoid_gate))
    d_gate = d_gate.astype(BF16)
    d_up = (d_hidden * gate * sigmoid_gate).astype(BF16)
    dn_part = (mul_right(d_gate, gate_w) + mul_right(d_up, up_w)).astype(BF16)
    hidden, d_gate, d_up, dn_part, mlp_low = join((hidden, d_gate, d_up, dn_part, mlp_low))
    dn_two = scatter(dn_part, CTX)

    def by_owner(grad):
        return grad.reshape((4, grad.shape[0] // 4) + grad.shape[1:])

    gate_parts = send_parts_dp(by_owner(mul_left(xn_two, d_gate)))
    d_up = after(d_up, gate_parts[0])
    up_parts = send_parts_dp(by_owner(mul_left(xn_two, d_up)))
    hidden = after(hidden, up_parts[0])
    down_parts = send_parts_dp(by_owner(mul_left(hidden, dy_all)))
    dn_two, gate_parts, up_parts[0], down_parts[0] = join(
        (dn_two, gate_parts, up_parts[0], down_parts[0])
    )
    gate_sum = add_parts(gate_parts).astype(BF16)

    d_res = cotangent[0].astype(F32) + norm_back(hid_res, nrm_two, dn_two)
    d_res_low = d_res.astype(BF16)
    d_attn = mul_right(d_res_low, output_w).astype(BF16)
    d_head = swap(d_attn.reshape(tok_rows, groups, HD).transpose(1, 0, 2), CTX)
    attn_o_two = flip(attn_o, "core")
    d_head, mlp_high, gate_sum, attn_o_two, d_res_low = join(
        (d_head, mlp_part[:, cut:], gate_sum, attn_o_two, d_res_low)
    )
    mlp_high = scatter(mlp_high, CTX)
    gate_sum = swap(gate_sum.reshape(groups, shard, slice_ff), CTX)
    d_res_two = flip(d_res_low, "core")
    d_head = d_head.reshape(span, HD)
    core = lax.axis_index("core")

    def own_columns(values):
        values = values.reshape(tok_rows, 16, 2, shard)
        return lax.dynamic_index_in_dim(values, core, 2, keepdims=False).reshape(tok_rows, -1)

    both_o = jnp.concatenate((own_columns(attn_o), own_columns(attn_o_two)), axis=0)
    both_d = jnp.concatenate((d_res_low, d_res_two), axis=0)
    output_part = mul_left(both_o, both_d).reshape(4, 4, shard, width)
    d_prob = mul_right(d_head, value)
    row_delta = jnp.sum(prob * d_prob, axis=-1, keepdims=True)
    d_score = (prob * (d_prob - row_delta)).astype(BF16)
    d_query = turn(mul_plain(d_score, key) * scale, -sine)
    d_key = turn(mul_left(d_score, query) * scale, -sine)
    d_value = mul_left(prob_low, d_head)
    d_qkv = jnp.concatenate((d_query, d_key, d_value), axis=1).astype(BF16)
    d_qkv, gate_sum, up_parts, output_part = join((d_qkv, gate_sum, up_parts, output_part))
    output_parts = send_parts_dp(output_part)
    up_sum = swap(add_parts(up_parts).astype(BF16).reshape(groups, shard, slice_ff), CTX)
    dn_part_one = mul_right(d_qkv, qkv_w).astype(BF16)
    dn_part_one, xn_one, d_qkv, mlp_high, down_parts = join(
        (dn_part_one, xn_one, d_qkv, mlp_high, down_parts)
    )
    dn_one = scatter(dn_part_one, CTX)
    result = hid_res + jnp.concatenate((mlp_low, mlp_high), axis=1)
    result = result.astype(BF16)[None]
    down_grad = add_parts(down_parts)

    qkv_parts = send_parts_dp(mul_left(xn_one, d_qkv).reshape(4, groups * shard, 3 * HD))
    column = add_parts(output_parts)
    chip = lax.axis_index(("half", "low"))
    output_grad = take(column, chip)
    for step in range(1, 4):
        block = take(column, (chip + step) % 4).astype(BF16)
        output_grad = output_grad + turn_chips(block, step).astype(F32)
    qkv_sum = add_parts(qkv_parts).astype(BF16)
    qkv_sum = swap(qkv_sum.reshape(groups, shard, 3 * HD), CTX)
    def ungated(summed):
        blocks = summed.astype(F32).reshape(groups, shard, 4, share)
        return blocks.transpose(1, 2, 0, 3).reshape(shard, FF)

    gate_sum, up_sum = ungated(gate_sum), ungated(up_sum)
    gain_two_grad = jnp.sum(w_gate * gate_sum + w_up * up_sum, axis=1)

    input_grad = d_res + norm_back(tok_in, normalize(tok_in), dn_one)
    input_grad = input_grad.astype(BF16)[None]
    qkv_sum = qkv_sum.astype(F32).transpose(1, 0, 2)
    q_sum = qkv_sum[:, :, :HD].reshape(shard, H * HD)

    def per_group(summed):
        return jnp.sum(summed.reshape(shard, KVH, per_key, HD), axis=2).reshape(shard, KVH * HD)

    k_sum = per_group(qkv_sum[:, :, HD : 2 * HD])
    v_sum = per_group(qkv_sum[:, :, 2 * HD :])
    gain_one_grad = (
        jnp.sum(w_query * q_sum, axis=1)
        + jnp.sum(w_key * k_sum, axis=1)
        + jnp.sum(w_value * v_sum, axis=1)
    )
    return (
        result,
        input_grad,
        gain_one_grad,
        gain_one * q_sum,
        gain_one * k_sum,
        gain_one * v_sum,
        output_grad,
        gain_two_grad,
        gain_two * gate_sum,
        gain_two * up_sum,
        down_grad,
    )


def solution(mesh):
    if dict(mesh.shape) == {"dp": 4, "ctx": 8}:
        body, dp, ctx = head_split, ("y", "x"), CTX
        mesh = Mesh(mesh.devices.reshape(2, 2, 2, 2, 2), dp + ctx)
    else:
        body, dp, ctx = gathered_weights, ("dp",), ("ctx",)
    rows, whole = P(dp + ctx), P(dp + ctx, None)
    acts = P(dp, ctx, None)
    in_specs = (acts, P(dp), rows, whole, whole, whole, whole, rows, whole, whole, whole, acts)
    out_specs = (acts, acts, rows, whole, whole, whole, whole, rows, whole, whole, whole)
    return jax.shard_map(
        body, mesh=mesh, in_specs=in_specs, out_specs=out_specs, check_vma=False
    )
```

```python
import jax
import jax.numpy as jnp
from jax import lax
from jax.sharding import Mesh
from jax.sharding import PartitionSpec as P

FF = 8192
H = 8
KVH = 4
HD = 256
KEYBLK = 512


EPS = 1e-06
THETA = 1000042.0
NEG = -1e30


def mul_plain(first_op, second_op):
    return jnp.dot(first_op, second_op, preferred_element_type=jnp.float32)


def mul_right(first_op, second_op):
    return lax.dot_general(
        first_op, second_op, (((1,), (1,)), ((), ())), preferred_element_type=jnp.float32
    )


def mul_left(first_op, second_op):
    return lax.dot_general(
        first_op, second_op, (((0,), (0,)), ((), ())), preferred_element_type=jnp.float32
    )


def normalize(values):
    return values * lax.rsqrt(jnp.mean(values * values, axis=-1, keepdims=True) + EPS)


def norm_back(values, normed, grad_normed):
    factor = lax.rsqrt(jnp.mean(values * values, axis=-1, keepdims=True) + EPS)
    return factor * (grad_normed - normed * jnp.mean(grad_normed * normed, axis=-1, keepdims=True))


def rotary(first_pos, length, head_dim):
    half_dim = head_dim // 2
    frequency = 1.0 / THETA ** (lax.iota(jnp.float32, half_dim) * (2.0 / head_dim))
    angles = (first_pos + lax.iota(jnp.int32, length)).astype(jnp.float32)[:, None] * frequency[
        None, :
    ]
    cosine = jnp.concatenate((jnp.cos(angles), jnp.cos(angles)), axis=1)
    sine_table = jnp.concatenate((jnp.sin(angles), jnp.sin(angles)), axis=1)
    return (cosine, sine_table)


def rotate(values, cosine, sine_table):
    half_dim = values.shape[-1] // 2
    rolled = jnp.concatenate((-values[..., half_dim:], values[..., :half_dim]), axis=-1)
    return values * cosine[:, None, :] + rolled * sine_table[:, None, :]


def gathered_weights(
    tokens,
    prefix,
    g_attn,
    w_query,
    w_key,
    w_value,
    w_output,
    g_mlp,
    w_gate,
    w_up,
    w_down,
    cotangent,
):
    tok_rows = tokens.shape[1]
    key_span = lax.axis_size("ctx") * tok_rows
    first_pos = lax.axis_index("ctx") * tok_rows
    head_group = H // KVH
    query_width = H * HD
    key_width = KVH * HD
    score_scale = HD ** (-0.5)
    key_blocks = key_span // KEYBLK
    prefix_len = prefix[0]
    tok_in = tokens[0].astype(jnp.float32)
    nrm_one = normalize(tok_in)
    cosine, sine_table = rotary(first_pos, tok_rows, HD)
    query_pos = first_pos + lax.iota(jnp.int32, tok_rows)

    def visible(key_first, length):
        key_pos = key_first + lax.iota(jnp.int32, length)
        return (key_pos[None, :] <= query_pos[:, None]) | (key_pos[None, :] < prefix_len)

    gain_piece = lax.all_gather(g_attn, ("dp", "ctx"), axis=0, tiled=True)
    query_piece = lax.all_gather(w_query, ("dp", "ctx"), axis=0, tiled=True)
    key_piece = lax.all_gather(w_key, ("dp", "ctx"), axis=0, tiled=True)
    value_piece = lax.all_gather(w_value, ("dp", "ctx"), axis=0, tiled=True)
    length = gain_piece.shape[0]
    scaled = (nrm_one * gain_piece.astype(jnp.float32)).astype(jnp.bfloat16)
    q_raw = mul_plain(scaled, query_piece)
    k_raw = mul_plain(scaled, key_piece)
    v_raw = mul_plain(scaled, value_piece)
    xn_one = scaled
    query_low = rotate(q_raw.reshape(tok_rows, H, HD), cosine, sine_table).astype(jnp.bfloat16)
    query_low = query_low.reshape(tok_rows, KVH, head_group, HD)
    key_low = (
        rotate(k_raw.reshape(tok_rows, KVH, HD), cosine, sine_table)
        .astype(jnp.bfloat16)
        .reshape(tok_rows, key_width)
    )
    value_low = v_raw.astype(jnp.bfloat16)
    key_all, value_all = (
        lax.all_gather(key_low, "ctx", axis=0, tiled=True),
        lax.all_gather(value_low, "ctx", axis=0, tiled=True),
    )
    keys_heads = key_all.reshape(key_span, KVH, HD)
    values_heads = value_all.reshape(key_span, KVH, HD)
    scores = (
        jnp.einsum("tkgd,skd->kgts", query_low, keys_heads, preferred_element_type=jnp.float32)
        * score_scale
    )
    scores = jnp.where(visible(0, key_span), scores, NEG)
    row_max = jnp.max(scores, axis=-1, keepdims=True)
    log_total = row_max + jnp.log(jnp.sum(jnp.exp(scores - row_max), axis=-1, keepdims=True))
    prob_low = jnp.exp(scores - log_total).astype(jnp.bfloat16)
    attn_o = jnp.einsum(
        "kgts,skd->tkgd", prob_low, values_heads, preferred_element_type=jnp.float32
    )
    attn_o = attn_o.reshape(tok_rows, query_width).astype(jnp.bfloat16)
    attn_out = mul_plain(attn_o, lax.all_gather(w_output, ("dp", "ctx"), axis=0, tiled=True))
    hid_res = tok_in + attn_out
    nrm_two = normalize(hid_res)
    gain_piece = lax.all_gather(g_mlp, ("dp", "ctx"), axis=0, tiled=True)
    gate_piece = lax.all_gather(w_gate, ("dp", "ctx"), axis=0, tiled=True)
    up_piece = lax.all_gather(w_up, ("dp", "ctx"), axis=0, tiled=True)
    length = gain_piece.shape[0]
    scaled = (nrm_two * gain_piece.astype(jnp.float32)).astype(jnp.bfloat16)
    gate = mul_plain(scaled, gate_piece)
    up_val = mul_plain(scaled, up_piece)
    sigmoid_gate = jax.nn.sigmoid(gate)
    hidden = (gate * sigmoid_gate * up_val).astype(jnp.bfloat16)
    mlp_out = mul_plain(hidden, lax.all_gather(w_down, ("dp", "ctx"), axis=0, tiled=True))
    result = (hid_res + mlp_out).astype(jnp.bfloat16)[None]
    grad_y = cotangent[0]
    grad_hidden = mul_right(grad_y, lax.all_gather(w_down, ("dp", "ctx"), axis=0, tiled=True))
    grad_gate_low = (
        grad_hidden * up_val * sigmoid_gate * (1.0 + gate * (1.0 - sigmoid_gate))
    ).astype(jnp.bfloat16)
    grad_up_low = (grad_hidden * gate * sigmoid_gate).astype(jnp.bfloat16)
    gain_piece = lax.all_gather(g_mlp, ("dp", "ctx"), axis=0, tiled=True)
    gate_piece = lax.all_gather(w_gate, ("dp", "ctx"), axis=0, tiled=True)
    up_piece = lax.all_gather(w_up, ("dp", "ctx"), axis=0, tiled=True)
    summed = mul_right(grad_gate_low, gate_piece) + mul_right(grad_up_low, up_piece)
    stacked = jnp.stack((summed * gain_piece.astype(jnp.float32), summed))
    mlp_pair = stacked
    gain_two_grad = jnp.sum(mlp_pair[1] * nrm_two, axis=0)
    d_res = grad_y.astype(jnp.float32) + norm_back(hid_res, nrm_two, mlp_pair[0])
    gate_up_low = jnp.concatenate((grad_gate_low, grad_up_low), axis=1)
    gate_up_grad = lax.psum_scatter(
        mul_left(scaled, gate_up_low), ("dp", "ctx"), scatter_dimension=0, tiled=True
    )
    down_grad = lax.psum_scatter(
        mul_left(hidden, grad_y), ("dp", "ctx"), scatter_dimension=0, tiled=True
    )
    d_res_low = d_res.astype(jnp.bfloat16)
    grad_attn = mul_right(d_res_low, lax.all_gather(w_output, ("dp", "ctx"), axis=0, tiled=True))
    grad_attn_low = grad_attn.astype(jnp.bfloat16).reshape(tok_rows, KVH, head_group, HD)

    def block_parts(block_id):
        key_first = block_id * KEYBLK
        key_block = lax.dynamic_slice_in_dim(keys_heads, key_first, KEYBLK, 0)
        value_block = lax.dynamic_slice_in_dim(values_heads, key_first, KEYBLK, 0)
        block_scores = (
            jnp.einsum("tkgd,skd->kgts", query_low, key_block, preferred_element_type=jnp.float32)
            * score_scale
        )
        block_scores = jnp.where(visible(key_first, KEYBLK), block_scores, NEG)
        prob_full = jnp.exp(block_scores - log_total)
        grad_prob = jnp.einsum(
            "tkgd,skd->kgts", grad_attn_low, value_block, preferred_element_type=jnp.float32
        )
        return (key_block, prob_full, grad_prob)

    def delta_step(summed, block_id):
        unused_keys, prob_full, grad_prob = block_parts(block_id)
        return (summed + jnp.sum(prob_full * grad_prob, axis=-1, keepdims=True), None)

    row_delta, unused_out = lax.scan(
        delta_step, jnp.zeros(log_total.shape, jnp.float32), lax.iota(jnp.int32, key_blocks)
    )

    def grad_step(grad_query, block_id):
        key_block, prob_full, grad_prob = block_parts(block_id)
        grad_score = (prob_full * (grad_prob - row_delta)).astype(jnp.bfloat16)
        grad_query = (
            grad_query
            + jnp.einsum(
                "kgts,skd->tkgd", grad_score, key_block, preferred_element_type=jnp.float32
            )
            * score_scale
        )
        grad_key_block = (
            jnp.einsum("kgts,tkgd->skd", grad_score, query_low, preferred_element_type=jnp.float32)
            * score_scale
        )
        grad_value_block = jnp.einsum(
            "kgts,tkgd->skd",
            prob_full.astype(jnp.bfloat16),
            grad_attn_low,
            preferred_element_type=jnp.float32,
        )
        return (
            grad_query,
            (
                grad_key_block.reshape(KEYBLK, key_width),
                grad_value_block.reshape(KEYBLK, key_width),
            ),
        )

    grad_query, block_grads = lax.scan(
        grad_step,
        jnp.zeros((tok_rows, KVH, head_group, HD), jnp.float32),
        lax.iota(jnp.int32, key_blocks),
    )
    keys_grad_all = block_grads[0].reshape(key_span, key_width)
    values_grad_all = block_grads[1].reshape(key_span, key_width)
    key_grad_own, value_grad_own = (
        lax.psum_scatter(
            keys_grad_all.astype(jnp.bfloat16), "ctx", scatter_dimension=0, tiled=True
        ).astype(jnp.float32),
        lax.psum_scatter(
            values_grad_all.astype(jnp.bfloat16), "ctx", scatter_dimension=0, tiled=True
        ).astype(jnp.float32),
    )
    query_grad_low = rotate(grad_query.reshape(tok_rows, H, HD), cosine, -sine_table).astype(
        jnp.bfloat16
    )
    query_grad_low = query_grad_low.reshape(tok_rows, query_width)
    key_grad_low = rotate(key_grad_own.reshape(tok_rows, KVH, HD), cosine, -sine_table).astype(
        jnp.bfloat16
    )
    key_grad_low = key_grad_low.reshape(tok_rows, key_width)
    value_grad_low = value_grad_own.astype(jnp.bfloat16)
    gain_piece = lax.all_gather(g_attn, ("dp", "ctx"), axis=0, tiled=True)
    query_piece = lax.all_gather(w_query, ("dp", "ctx"), axis=0, tiled=True)
    key_piece = lax.all_gather(w_key, ("dp", "ctx"), axis=0, tiled=True)
    value_piece = lax.all_gather(w_value, ("dp", "ctx"), axis=0, tiled=True)
    summed = (
        mul_right(query_grad_low, query_piece)
        + mul_right(key_grad_low, key_piece)
        + mul_right(value_grad_low, value_piece)
    )
    stacked = jnp.stack((summed * gain_piece.astype(jnp.float32), summed))
    gain_one_grad = jnp.sum(stacked[1] * nrm_one, axis=0)
    input_grad = (d_res + norm_back(tok_in, nrm_one, stacked[0])).astype(jnp.bfloat16)[None]
    qkv_grad_low = jnp.concatenate((query_grad_low, key_grad_low, value_grad_low), axis=1)
    first_part = mul_left(xn_one, qkv_grad_low)
    second_part = mul_left(attn_o, d_res_low)
    attn_grad = lax.psum_scatter(
        jnp.concatenate((first_part, second_part), axis=1),
        ("dp", "ctx"),
        scatter_dimension=0,
        tiled=True,
    )
    gain_grads = (
        lax.psum_scatter(gain_one_grad, ("dp", "ctx"), scatter_dimension=0, tiled=True),
        lax.psum_scatter(gain_two_grad, ("dp", "ctx"), scatter_dimension=0, tiled=True),
    )
    return (
        result,
        input_grad,
        gain_grads[0],
        attn_grad[:, :query_width],
        attn_grad[:, query_width : query_width + key_width],
        attn_grad[:, query_width + key_width : query_width + 2 * key_width],
        attn_grad[:, query_width + 2 * key_width :],
        gain_grads[1],
        gate_up_grad[:, :FF],
        gate_up_grad[:, FF:],
        down_grad,
    )


BF16, F32 = jnp.bfloat16, jnp.float32
CTX = ("half", "low", "core")
TEAM = ("x", "low", "core")
join = lax.optimization_barrier


def put(buffer, block, index):
    return lax.dynamic_update_slice(buffer, block[None], (index,) + (0,) * block.ndim)


def take(values, index):
    return lax.dynamic_index_in_dim(values, index, 0, keepdims=False)


def after(values, *others):
    return join((values,) + others)[0]


def flip(values, axis, bits=1):
    return lax.ppermute(values, axis, [(i, i ^ bits) for i in range(lax.axis_size(axis))])


def send_dp(own):
    return [own] + [flip(own, ("y", "x"), bits) for bits in range(1, 4)]


def order_dp(blocks):
    d = lax.axis_index(("y", "x"))
    buffer = jnp.zeros((4,) + blocks[0].shape, blocks[0].dtype)
    for bits, block in enumerate(blocks):
        buffer = put(buffer, block, d ^ bits)
    return buffer


def split_parts_dp(parts):
    d = lax.axis_index(("y", "x"))
    return [take(parts, d ^ bits) for bits in range(4)]


def send_parts_dp(split, bits=(1, 2, 3)):
    return [flip(split[b], ("y", "x"), b) for b in bits]


def add_parts(parts):
    total = parts[0].astype(F32)
    for part in parts[1:]:
        total = total + part.astype(F32)
    return total


def turn_chips(values, step):
    pairs = [(c, (c + 2 * step) % 8) for c in range(8)]
    return lax.ppermute(values, CTX, pairs)


def send_column(rows):
    return [rows] + [turn_chips(rows, step) for step in range(1, 4)]


def order_column(blocks):
    chip = lax.axis_index(("half", "low"))
    column = jnp.zeros((4,) + blocks[0].shape, blocks[0].dtype)
    for step, block in enumerate(blocks):
        column = put(column, block, (chip - step) % 4)
    return column


def order_cores(mine, other):
    core = lax.axis_index("core")
    low, high = jnp.where(core == 0, mine, other), jnp.where(core == 0, other, mine)
    return jnp.stack((low, high), axis=-3)


def order_teams(near, far, near_y, far_y):
    y, half = lax.axis_index("y"), lax.axis_index("half")
    buffer = jnp.zeros((4,) + near.shape, near.dtype)
    for block, bits in ((near, 0), (far, 1), (near_y, 2), (far_y, 3)):
        buffer = put(buffer, block, (2 * y + half) ^ bits)
    return buffer.reshape((2, 2) + near.shape)


def swap(values, axes):
    return lax.all_to_all(values, axes, split_axis=0, concat_axis=0, tiled=True)


def swap_steps(values):
    chip, core = lax.axis_index(("half", "low")), lax.axis_index("core")
    values = values.reshape((4, 2) + values.shape[1:])
    got = [take(values, chip)]
    got += [turn_chips(take(values, (chip + step) % 4), step) for step in range(1, 4)]
    column = order_column(got)
    mine = lax.dynamic_index_in_dim(column, core, 1, keepdims=False)
    other = flip(lax.dynamic_index_in_dim(column, 1 - core, 1, keepdims=False), "core")
    low, high = jnp.where(core == 0, mine, other), jnp.where(core == 0, other, mine)
    return jnp.stack((low, high), axis=1).reshape((8,) + values.shape[2:])


def gather(values, axes):
    return lax.all_gather(values, axes, axis=0, tiled=True)


def scatter(values, axes):
    return lax.psum_scatter(values, axes, scatter_dimension=0, tiled=True).astype(F32)


def other_y(parts):
    return flip(take(parts, 1 - lax.axis_index("y")).astype(BF16), "y")


def add_y(parts, got):
    return take(parts, lax.axis_index("y")) + got.astype(F32)


def other_half(parts):
    return flip(take(parts, 1 - lax.axis_index("half")).astype(BF16), "half")


def add_half(parts, got):
    return take(parts, lax.axis_index("half")) + got.astype(F32)


def head_split(
    tokens,
    prefix,
    g_attn,
    w_query,
    w_key,
    w_value,
    w_output,
    g_mlp,
    w_gate,
    w_up,
    w_down,
    cotangent,
):
    groups = 8
    tok_rows, width = tokens.shape[1:]
    span = groups * tok_rows
    shard = w_query.shape[0]
    share = w_down.shape[0]
    slice_ff = 4 * share
    per_key = H // KVH
    scale = HD ** (-0.5)

    tok_in = tokens[0].astype(F32)
    gain_one, gain_two = g_attn.astype(F32)[:, None], g_mlp.astype(F32)[:, None]

    q_cols = (gain_one * w_query).astype(BF16).reshape(shard, H, HD)
    k_cols = jnp.repeat((gain_one * w_key).astype(BF16).reshape(shard, KVH, HD), per_key, axis=1)
    v_cols = jnp.repeat((gain_one * w_value).astype(BF16).reshape(shard, KVH, HD), per_key, axis=1)
    qkv_cols = jnp.concatenate((q_cols, k_cols, v_cols), axis=2).transpose(1, 0, 2)

    def gated(weight):
        scaled = (gain_two * weight).astype(BF16).reshape(shard, 4, groups, share)
        return scaled.transpose(2, 0, 1, 3).reshape(groups, shard, slice_ff)

    gate_cols, up_cols = gated(w_gate), gated(w_up)
    cosine, sine = rotary(0, span, HD)

    def turn(values, sine_table):
        half = HD // 2
        rolled = jnp.concatenate((-values[:, half:], values[:, :half]), axis=-1)
        return values * cosine + rolled * sine_table

    down_blocks = send_dp(w_down)
    tok_all = gather(tokens[0], CTX)
    qkv_rows = swap(qkv_cols, CTX).reshape(groups * shard, 3 * HD)
    qkv_rows, out_own, gate_cols, up_cols = join((qkv_rows, w_output, gate_cols, up_cols))
    qkv_blocks = send_dp(qkv_rows)
    out_blocks = send_column(out_own)
    qkv_w = order_dp(qkv_blocks).reshape(width, 3 * HD)
    out_rows = order_column(out_blocks)
    down_w = order_dp(down_blocks).reshape(slice_ff, width)
    tok_all, qkv_w, down_w, gate_cols, cosine, sine = join(
        (tok_all, qkv_w, down_w, gate_cols, cosine, sine)
    )
    cut = width // 2
    dy_left = gather(after(cotangent[0][:, :cut], tok_all), CTX)
    out_mine = order_dp(send_dp(after(out_rows, qkv_w)))
    gate_rows = swap(gate_cols, CTX).reshape(groups * shard, slice_ff)
    xn_one = normalize(tok_all.astype(F32)).astype(BF16)
    qkv = mul_plain(xn_one, qkv_w)
    query = turn(qkv[:, :HD], sine).astype(BF16)
    key = turn(qkv[:, HD : 2 * HD], sine).astype(BF16)
    value = qkv[:, 2 * HD :].astype(BF16)
    query, key, value, gate_rows, up_cols, out_mine = join(
        (query, key, value, gate_rows, up_cols, out_mine)
    )
    gate_w = gather(gate_rows, ("y", "x"))
    up_rows = swap(up_cols, CTX).reshape(groups * shard, slice_ff)
    scores = mul_right(query, key) * scale
    pos = lax.iota(jnp.int32, span)
    seen = (pos[None, :] <= pos[:, None]) | (pos[None, :] < prefix[0])
    scores = jnp.where(seen, scores, NEG)
    prob = jax.nn.softmax(scores, axis=-1)
    prob_low = prob.astype(BF16)
    head_o = mul_plain(prob_low, value).astype(BF16)
    head_o, up_rows = join((head_o, up_rows))
    attn_o = swap(head_o.reshape(groups, tok_rows, HD), CTX)
    output_w = order_cores(out_mine, flip(out_mine, "core")).reshape(H * HD, width)
    attn_o, output_w = join((attn_o, output_w))
    up_blocks = send_dp(up_rows)
    attn_o = attn_o.transpose(1, 0, 2).reshape(tok_rows, H * HD)
    hid_res = tok_in + mul_plain(attn_o, output_w)
    nrm_two = normalize(hid_res)
    xn_two = gather(nrm_two.astype(BF16), CTX)
    up_w = order_dp(up_blocks).reshape(width, slice_ff)
    xn_two, gate_w, up_w, dy_left, dy_own = join(
        (xn_two, gate_w, up_w, dy_left, cotangent[0][:, cut:])
    )
    dy_right = gather(dy_own, CTX)
    gate, up_val = mul_plain(xn_two, gate_w), mul_plain(xn_two, up_w)
    sigmoid_gate = jax.nn.sigmoid(gate)
    hidden = (gate * sigmoid_gate * up_val).astype(BF16)
    mlp_part = mul_plain(hidden, down_w).astype(BF16)
    mlp_part, gate, up_val, dy_right = join((mlp_part, gate, up_val, dy_right))
    mlp_sum = scatter(mlp_part, CTX)
    sigmoid_gate = jax.nn.sigmoid(gate)
    d_hidden = mul_right(dy_left, down_w[:, :cut]) + mul_right(dy_right, down_w[:, cut:])
    d_gate = d_hidden * up_val * sigmoid_gate * (1.0 + gate * (1.0 - sigmoid_gate))
    d_gate = d_gate.astype(BF16)
    d_up = (d_hidden * gate * sigmoid_gate).astype(BF16)

    def by_owner(grad):
        return grad.reshape((4, grad.shape[0] // 4) + grad.shape[1:])

    gate_split = split_parts_dp(by_owner(mul_left(xn_two, d_gate).astype(BF16)))
    up_split = split_parts_dp(by_owner(mul_left(xn_two, d_up).astype(BF16)))
    hidden, d_gate, d_up, gate_split, up_split = join(
        (hidden, d_gate, d_up, gate_split, up_split)
    )
    gate_near = send_parts_dp(gate_split, (1, 2))
    dn_part = (mul_right(d_gate, gate_w) + mul_right(d_up, up_w)).astype(BF16)
    hidden, dn_part, mlp_sum, gate_near, gate_split, up_split = join(
        (hidden, dn_part, mlp_sum, gate_near, gate_split, up_split)
    )
    gate_up_far = send_parts_dp(gate_split, (3,)) + send_parts_dp(up_split)
    dn_two = scatter(dn_part, CTX)
    down_split = [
        split_parts_dp(by_owner(mul_left(hidden, part).astype(BF16))) for part in (dy_left, dy_right)
    ]
    dn_two, gate_up_far, down_split = join((dn_two, gate_up_far, down_split))
    d_res = cotangent[0].astype(F32) + norm_back(hid_res, nrm_two, dn_two)
    d_res_low = d_res.astype(BF16)
    d_attn = mul_right(d_res_low, output_w).astype(BF16)
    d_head = swap(d_attn.reshape(tok_rows, groups, HD).transpose(1, 0, 2), CTX)
    attn_o_two, d_res_two = flip(attn_o, "core"), flip(d_res_low, "core")
    core = lax.axis_index("core")

    def own_columns(values):
        values = values.reshape(tok_rows, 16, 2, shard)
        return lax.dynamic_index_in_dim(values, core, 2, keepdims=False).reshape(tok_rows, -1)

    both_o = jnp.concatenate((own_columns(attn_o), own_columns(attn_o_two)), axis=0)
    both_d = jnp.concatenate((d_res_low, d_res_two), axis=0)
    output_part = mul_left(both_o, both_d).astype(BF16).reshape(4, 4, shard, width)
    output_split = split_parts_dp(output_part)
    gate_parts = gate_split[:1] + gate_near + gate_up_far[:1]
    up_parts = up_split[:1] + gate_up_far[1:]
    gate_up_sum = jnp.stack([add_parts(parts).astype(BF16) for parts in (gate_parts, up_parts)])
    d_head, gate_up_sum, output_split = join((d_head, gate_up_sum, output_split))
    output_parts = output_split[:1] + send_parts_dp(output_split)
    gate_up_sum = gate_up_sum.reshape(2, groups, shard, slice_ff)
    gate_up_sum = lax.all_to_all(gate_up_sum, CTX, split_axis=1, concat_axis=1, tiled=True)
    d_head = d_head.reshape(span, HD)
    d_prob = mul_right(d_head, value)
    row_delta = jnp.sum(prob * d_prob, axis=-1, keepdims=True)
    d_score = (prob * (d_prob - row_delta)).astype(BF16)
    d_query = turn(mul_plain(d_score, key) * scale, -sine)
    d_key = turn(mul_left(d_score, query) * scale, -sine)
    d_value = mul_left(prob_low, d_head)
    d_qkv = jnp.concatenate((d_query, d_key, d_value), axis=1).astype(BF16)
    d_qkv, gate_up_sum, output_parts = join((d_qkv, gate_up_sum, output_parts))
    gate_sum, up_sum = gate_up_sum[0], gate_up_sum[1]
    dn_part_one = mul_right(d_qkv, qkv_w).astype(BF16)
    dn_part_one, xn_one, d_qkv, mlp_sum = join((dn_part_one, xn_one, d_qkv, mlp_sum))
    dn_one = scatter(dn_part_one, CTX)
    result = (hid_res + mlp_sum).astype(BF16)[None]

    qkv_split = split_parts_dp(
        mul_left(xn_one, d_qkv).astype(BF16).reshape(4, groups * shard, 3 * HD)
    )
    qkv_parts = qkv_split[:1] + send_parts_dp(qkv_split)
    column = add_parts(output_parts)
    chip = lax.axis_index(("half", "low"))
    output_parts = [take(column, chip)]
    for step in range(1, 4):
        block = take(column, (chip + step) % 4).astype(BF16)
        output_parts.append(turn_chips(block, step))
    qkv_parts, output_parts, down_split = join((qkv_parts, output_parts, down_split))
    qkv_sum = add_parts(qkv_parts).astype(BF16)
    qkv_sum = swap(qkv_sum.reshape(groups, shard, 3 * HD), CTX)
    output_grad = add_parts(output_parts)
    down_parts = [split[:1] + send_parts_dp(split) for split in down_split]
    down_grad = jnp.concatenate([add_parts(parts) for parts in down_parts], axis=1)

    def ungated(summed):
        blocks = summed.astype(F32).reshape(groups, shard, 4, share)
        return blocks.transpose(1, 2, 0, 3).reshape(shard, FF)

    gate_sum, up_sum = ungated(gate_sum), ungated(up_sum)
    gain_two_grad = jnp.sum(w_gate * gate_sum + w_up * up_sum, axis=1)

    input_grad = d_res + norm_back(tok_in, normalize(tok_in), dn_one)
    input_grad = input_grad.astype(BF16)[None]
    qkv_sum = qkv_sum.astype(F32).transpose(1, 0, 2)
    q_sum = qkv_sum[:, :, :HD].reshape(shard, H * HD)

    def per_group(summed):
        return jnp.sum(summed.reshape(shard, KVH, per_key, HD), axis=2).reshape(shard, KVH * HD)

    k_sum = per_group(qkv_sum[:, :, HD : 2 * HD])
    v_sum = per_group(qkv_sum[:, :, 2 * HD :])
    gain_one_grad = (
        jnp.sum(w_query * q_sum, axis=1)
        + jnp.sum(w_key * k_sum, axis=1)
        + jnp.sum(w_value * v_sum, axis=1)
    )
    return (
        result,
        input_grad,
        gain_one_grad,
        gain_one * q_sum,
        gain_one * k_sum,
        gain_one * v_sum,
        output_grad,
        gain_two_grad,
        gain_two * gate_sum,
        gain_two * up_sum,
        down_grad,
    )


def solution(mesh):
    if dict(mesh.shape) == {"dp": 4, "ctx": 8}:
        body, dp, ctx = head_split, ("y", "x"), CTX
        mesh = Mesh(mesh.devices.reshape(2, 2, 2, 2, 2), dp + ctx)
    else:
        body, dp, ctx = gathered_weights, ("dp",), ("ctx",)
    rows, whole = P(dp + ctx), P(dp + ctx, None)
    acts = P(dp, ctx, None)
    in_specs = (acts, P(dp), rows, whole, whole, whole, whole, rows, whole, whole, whole, acts)
    out_specs = (acts, acts, rows, whole, whole, whole, whole, rows, whole, whole, whole)
    return jax.shard_map(
        body, mesh=mesh, in_specs=in_specs, out_specs=out_specs, check_vma=False
    )
```

```python
import jax
import jax.numpy as jnp
from jax import lax
from jax.experimental import pallas as pl
from jax.experimental.pallas import tpu as pltpu
from jax.sharding import Mesh
from jax.sharding import PartitionSpec as P

FF = 8192
H = 8
KVH = 4
HD = 256
KEYBLK = 512


EPS = 1e-06
THETA = 1000042.0
NEG = -1e30


def mul_plain(first_op, second_op):
    return jnp.dot(first_op, second_op, preferred_element_type=jnp.float32)


def mul_right(first_op, second_op):
    return lax.dot_general(
        first_op, second_op, (((1,), (1,)), ((), ())), preferred_element_type=jnp.float32
    )


def mul_left(first_op, second_op):
    return lax.dot_general(
        first_op, second_op, (((0,), (0,)), ((), ())), preferred_element_type=jnp.float32
    )


def normalize(values):
    return values * lax.rsqrt(jnp.mean(values * values, axis=-1, keepdims=True) + EPS)


def norm_back(values, normed, grad_normed):
    factor = lax.rsqrt(jnp.mean(values * values, axis=-1, keepdims=True) + EPS)
    return factor * (grad_normed - normed * jnp.mean(grad_normed * normed, axis=-1, keepdims=True))


def rotary(first_pos, length, head_dim):
    half_dim = head_dim // 2
    frequency = 1.0 / THETA ** (lax.iota(jnp.float32, half_dim) * (2.0 / head_dim))
    angles = (first_pos + lax.iota(jnp.int32, length)).astype(jnp.float32)[:, None] * frequency[
        None, :
    ]
    cosine = jnp.concatenate((jnp.cos(angles), jnp.cos(angles)), axis=1)
    sine_table = jnp.concatenate((jnp.sin(angles), jnp.sin(angles)), axis=1)
    return (cosine, sine_table)


def rotate(values, cosine, sine_table):
    half_dim = values.shape[-1] // 2
    rolled = jnp.concatenate((-values[..., half_dim:], values[..., :half_dim]), axis=-1)
    return values * cosine[:, None, :] + rolled * sine_table[:, None, :]


def gathered_weights(
    tokens,
    prefix,
    g_attn,
    w_query,
    w_key,
    w_value,
    w_output,
    g_mlp,
    w_gate,
    w_up,
    w_down,
    cotangent,
):
    tok_rows = tokens.shape[1]
    key_span = lax.axis_size("ctx") * tok_rows
    first_pos = lax.axis_index("ctx") * tok_rows
    head_group = H // KVH
    query_width = H * HD
    key_width = KVH * HD
    score_scale = HD ** (-0.5)
    key_blocks = key_span // KEYBLK
    prefix_len = prefix[0]
    tok_in = tokens[0].astype(jnp.float32)
    nrm_one = normalize(tok_in)
    cosine, sine_table = rotary(first_pos, tok_rows, HD)
    query_pos = first_pos + lax.iota(jnp.int32, tok_rows)

    def visible(key_first, length):
        key_pos = key_first + lax.iota(jnp.int32, length)
        return (key_pos[None, :] <= query_pos[:, None]) | (key_pos[None, :] < prefix_len)

    gain_piece = lax.all_gather(g_attn, ("dp", "ctx"), axis=0, tiled=True)
    query_piece = lax.all_gather(w_query, ("dp", "ctx"), axis=0, tiled=True)
    key_piece = lax.all_gather(w_key, ("dp", "ctx"), axis=0, tiled=True)
    value_piece = lax.all_gather(w_value, ("dp", "ctx"), axis=0, tiled=True)
    length = gain_piece.shape[0]
    scaled = (nrm_one * gain_piece.astype(jnp.float32)).astype(jnp.bfloat16)
    q_raw = mul_plain(scaled, query_piece)
    k_raw = mul_plain(scaled, key_piece)
    v_raw = mul_plain(scaled, value_piece)
    xn_one = scaled
    query_low = rotate(q_raw.reshape(tok_rows, H, HD), cosine, sine_table).astype(jnp.bfloat16)
    query_low = query_low.reshape(tok_rows, KVH, head_group, HD)
    key_low = (
        rotate(k_raw.reshape(tok_rows, KVH, HD), cosine, sine_table)
        .astype(jnp.bfloat16)
        .reshape(tok_rows, key_width)
    )
    value_low = v_raw.astype(jnp.bfloat16)
    key_all, value_all = (
        lax.all_gather(key_low, "ctx", axis=0, tiled=True),
        lax.all_gather(value_low, "ctx", axis=0, tiled=True),
    )
    keys_heads = key_all.reshape(key_span, KVH, HD)
    values_heads = value_all.reshape(key_span, KVH, HD)
    scores = (
        jnp.einsum("tkgd,skd->kgts", query_low, keys_heads, preferred_element_type=jnp.float32)
        * score_scale
    )
    scores = jnp.where(visible(0, key_span), scores, NEG)
    row_max = jnp.max(scores, axis=-1, keepdims=True)
    log_total = row_max + jnp.log(jnp.sum(jnp.exp(scores - row_max), axis=-1, keepdims=True))
    prob_low = jnp.exp(scores - log_total).astype(jnp.bfloat16)
    attn_o = jnp.einsum(
        "kgts,skd->tkgd", prob_low, values_heads, preferred_element_type=jnp.float32
    )
    attn_o = attn_o.reshape(tok_rows, query_width).astype(jnp.bfloat16)
    attn_out = mul_plain(attn_o, lax.all_gather(w_output, ("dp", "ctx"), axis=0, tiled=True))
    hid_res = tok_in + attn_out
    nrm_two = normalize(hid_res)
    gain_piece = lax.all_gather(g_mlp, ("dp", "ctx"), axis=0, tiled=True)
    gate_piece = lax.all_gather(w_gate, ("dp", "ctx"), axis=0, tiled=True)
    up_piece = lax.all_gather(w_up, ("dp", "ctx"), axis=0, tiled=True)
    length = gain_piece.shape[0]
    scaled = (nrm_two * gain_piece.astype(jnp.float32)).astype(jnp.bfloat16)
    gate = mul_plain(scaled, gate_piece)
    up_val = mul_plain(scaled, up_piece)
    sigmoid_gate = jax.nn.sigmoid(gate)
    hidden = (gate * sigmoid_gate * up_val).astype(jnp.bfloat16)
    mlp_out = mul_plain(hidden, lax.all_gather(w_down, ("dp", "ctx"), axis=0, tiled=True))
    result = (hid_res + mlp_out).astype(jnp.bfloat16)[None]
    grad_y = cotangent[0]
    grad_hidden = mul_right(grad_y, lax.all_gather(w_down, ("dp", "ctx"), axis=0, tiled=True))
    grad_gate_low = (
        grad_hidden * up_val * sigmoid_gate * (1.0 + gate * (1.0 - sigmoid_gate))
    ).astype(jnp.bfloat16)
    grad_up_low = (grad_hidden * gate * sigmoid_gate).astype(jnp.bfloat16)
    gain_piece = lax.all_gather(g_mlp, ("dp", "ctx"), axis=0, tiled=True)
    gate_piece = lax.all_gather(w_gate, ("dp", "ctx"), axis=0, tiled=True)
    up_piece = lax.all_gather(w_up, ("dp", "ctx"), axis=0, tiled=True)
    summed = mul_right(grad_gate_low, gate_piece) + mul_right(grad_up_low, up_piece)
    stacked = jnp.stack((summed * gain_piece.astype(jnp.float32), summed))
    mlp_pair = stacked
    gain_two_grad = jnp.sum(mlp_pair[1] * nrm_two, axis=0)
    d_res = grad_y.astype(jnp.float32) + norm_back(hid_res, nrm_two, mlp_pair[0])
    gate_up_low = jnp.concatenate((grad_gate_low, grad_up_low), axis=1)
    gate_up_grad = lax.psum_scatter(
        mul_left(scaled, gate_up_low), ("dp", "ctx"), scatter_dimension=0, tiled=True
    )
    down_grad = lax.psum_scatter(
        mul_left(hidden, grad_y), ("dp", "ctx"), scatter_dimension=0, tiled=True
    )
    d_res_low = d_res.astype(jnp.bfloat16)
    grad_attn = mul_right(d_res_low, lax.all_gather(w_output, ("dp", "ctx"), axis=0, tiled=True))
    grad_attn_low = grad_attn.astype(jnp.bfloat16).reshape(tok_rows, KVH, head_group, HD)

    def block_parts(block_id):
        key_first = block_id * KEYBLK
        key_block = lax.dynamic_slice_in_dim(keys_heads, key_first, KEYBLK, 0)
        value_block = lax.dynamic_slice_in_dim(values_heads, key_first, KEYBLK, 0)
        block_scores = (
            jnp.einsum("tkgd,skd->kgts", query_low, key_block, preferred_element_type=jnp.float32)
            * score_scale
        )
        block_scores = jnp.where(visible(key_first, KEYBLK), block_scores, NEG)
        prob_full = jnp.exp(block_scores - log_total)
        grad_prob = jnp.einsum(
            "tkgd,skd->kgts", grad_attn_low, value_block, preferred_element_type=jnp.float32
        )
        return (key_block, prob_full, grad_prob)

    def delta_step(summed, block_id):
        unused_keys, prob_full, grad_prob = block_parts(block_id)
        return (summed + jnp.sum(prob_full * grad_prob, axis=-1, keepdims=True), None)

    row_delta, unused_out = lax.scan(
        delta_step, jnp.zeros(log_total.shape, jnp.float32), lax.iota(jnp.int32, key_blocks)
    )

    def grad_step(grad_query, block_id):
        key_block, prob_full, grad_prob = block_parts(block_id)
        grad_score = (prob_full * (grad_prob - row_delta)).astype(jnp.bfloat16)
        grad_query = (
            grad_query
            + jnp.einsum(
                "kgts,skd->tkgd", grad_score, key_block, preferred_element_type=jnp.float32
            )
            * score_scale
        )
        grad_key_block = (
            jnp.einsum("kgts,tkgd->skd", grad_score, query_low, preferred_element_type=jnp.float32)
            * score_scale
        )
        grad_value_block = jnp.einsum(
            "kgts,tkgd->skd",
            prob_full.astype(jnp.bfloat16),
            grad_attn_low,
            preferred_element_type=jnp.float32,
        )
        return (
            grad_query,
            (
                grad_key_block.reshape(KEYBLK, key_width),
                grad_value_block.reshape(KEYBLK, key_width),
            ),
        )

    grad_query, block_grads = lax.scan(
        grad_step,
        jnp.zeros((tok_rows, KVH, head_group, HD), jnp.float32),
        lax.iota(jnp.int32, key_blocks),
    )
    keys_grad_all = block_grads[0].reshape(key_span, key_width)
    values_grad_all = block_grads[1].reshape(key_span, key_width)
    key_grad_own, value_grad_own = (
        lax.psum_scatter(
            keys_grad_all.astype(jnp.bfloat16), "ctx", scatter_dimension=0, tiled=True
        ).astype(jnp.float32),
        lax.psum_scatter(
            values_grad_all.astype(jnp.bfloat16), "ctx", scatter_dimension=0, tiled=True
        ).astype(jnp.float32),
    )
    query_grad_low = rotate(grad_query.reshape(tok_rows, H, HD), cosine, -sine_table).astype(
        jnp.bfloat16
    )
    query_grad_low = query_grad_low.reshape(tok_rows, query_width)
    key_grad_low = rotate(key_grad_own.reshape(tok_rows, KVH, HD), cosine, -sine_table).astype(
        jnp.bfloat16
    )
    key_grad_low = key_grad_low.reshape(tok_rows, key_width)
    value_grad_low = value_grad_own.astype(jnp.bfloat16)
    gain_piece = lax.all_gather(g_attn, ("dp", "ctx"), axis=0, tiled=True)
    query_piece = lax.all_gather(w_query, ("dp", "ctx"), axis=0, tiled=True)
    key_piece = lax.all_gather(w_key, ("dp", "ctx"), axis=0, tiled=True)
    value_piece = lax.all_gather(w_value, ("dp", "ctx"), axis=0, tiled=True)
    summed = (
        mul_right(query_grad_low, query_piece)
        + mul_right(key_grad_low, key_piece)
        + mul_right(value_grad_low, value_piece)
    )
    stacked = jnp.stack((summed * gain_piece.astype(jnp.float32), summed))
    gain_one_grad = jnp.sum(stacked[1] * nrm_one, axis=0)
    input_grad = (d_res + norm_back(tok_in, nrm_one, stacked[0])).astype(jnp.bfloat16)[None]
    qkv_grad_low = jnp.concatenate((query_grad_low, key_grad_low, value_grad_low), axis=1)
    first_part = mul_left(xn_one, qkv_grad_low)
    second_part = mul_left(attn_o, d_res_low)
    attn_grad = lax.psum_scatter(
        jnp.concatenate((first_part, second_part), axis=1),
        ("dp", "ctx"),
        scatter_dimension=0,
        tiled=True,
    )
    gain_grads = (
        lax.psum_scatter(gain_one_grad, ("dp", "ctx"), scatter_dimension=0, tiled=True),
        lax.psum_scatter(gain_two_grad, ("dp", "ctx"), scatter_dimension=0, tiled=True),
    )
    return (
        result,
        input_grad,
        gain_grads[0],
        attn_grad[:, :query_width],
        attn_grad[:, query_width : query_width + key_width],
        attn_grad[:, query_width + key_width : query_width + 2 * key_width],
        attn_grad[:, query_width + 2 * key_width :],
        gain_grads[1],
        gate_up_grad[:, :FF],
        gate_up_grad[:, FF:],
        down_grad,
    )


BF16, F32 = jnp.bfloat16, jnp.float32
CTX = ("half", "low", "core")
join = lax.optimization_barrier


def put(buffer, block, index):
    return lax.dynamic_update_slice(buffer, block[None], (index,) + (0,) * block.ndim)


def take(values, index):
    return lax.dynamic_index_in_dim(values, index, 0, keepdims=False)


def after(values, *others):
    return join((values,) + others)[0]


def flip(values, axis, bits=1):
    return lax.ppermute(values, axis, [(i, i ^ bits) for i in range(lax.axis_size(axis))])


def send_dp(own):
    return [own] + [flip(own, ("y", "x"), bits) for bits in range(1, 4)]


def order_dp(blocks):
    d = lax.axis_index(("y", "x"))
    buffer = jnp.zeros((4,) + blocks[0].shape, blocks[0].dtype)
    for bits, block in enumerate(blocks):
        buffer = put(buffer, block, d ^ bits)
    return buffer


def split_parts_dp(parts):
    d = lax.axis_index(("y", "x"))
    return [take(parts, d ^ bits) for bits in range(4)]


def send_parts_dp(split, bits=(1, 2, 3)):
    return [flip(split[b], ("y", "x"), b) for b in bits]


def add_parts(parts):
    total = parts[0].astype(F32)
    for part in parts[1:]:
        total = total + part.astype(F32)
    return total


def turn_chips(values, step):
    pairs = [(c, (c + 2 * step) % 8) for c in range(8)]
    return lax.ppermute(values, CTX, pairs)


def send_column(rows, steps=(1, 2, 3)):
    return [turn_chips(rows, step) for step in steps]


def order_column(blocks):
    chip = lax.axis_index(("half", "low"))
    column = jnp.zeros((4,) + blocks[0].shape, blocks[0].dtype)
    for step, block in enumerate(blocks):
        column = put(column, block, (chip - step) % 4)
    return column


def order_cores(mine, other):
    core = lax.axis_index("core")
    low, high = jnp.where(core == 0, mine, other), jnp.where(core == 0, other, mine)
    return jnp.stack((low, high), axis=-3)


def swap(values, axes):
    return lax.all_to_all(values, axes, split_axis=0, concat_axis=0, tiled=True)


def gather(values, axes):
    return lax.all_gather(values, axes, axis=0, tiled=True)


def scatter(values, axes):
    return lax.psum_scatter(values, axes, scatter_dimension=0, tiled=True).astype(F32)


BLOCK = 512


def attention_back_kernel(
    prefix_ref,
    query_ref,
    key_ref,
    value_ref,
    grad_ref,
    log_ref,
    delta_ref,
    cosine_ref,
    sine_ref,
    out_ref,
    dq_ref,
    dk_ref,
    dv_ref,
):
    steps = query_ref.shape[0] // BLOCK
    prefix = prefix_ref[0]
    scale = HD ** (-0.5)
    dq_ref[...] = jnp.zeros_like(dq_ref)
    dk_ref[...] = jnp.zeros_like(dk_ref)
    dv_ref[...] = jnp.zeros_like(dv_ref)
    row = lax.broadcasted_iota(jnp.int32, (BLOCK, BLOCK), 0)
    column = lax.broadcasted_iota(jnp.int32, (BLOCK, BLOCK), 1)

    def query_step(i, carry):
        here = pl.ds(pl.multiple_of(i * BLOCK, BLOCK), BLOCK)
        query, grad = query_ref[here, :], grad_ref[here, :]
        log_total, delta = log_ref[i], delta_ref[i]

        def key_step(j, carry):
            there = pl.ds(pl.multiple_of(j * BLOCK, BLOCK), BLOCK)
            key, value = key_ref[there, :], value_ref[there, :]
            key_pos, query_pos = j * BLOCK + row, i * BLOCK + column
            seen = (key_pos <= query_pos) | (key_pos < prefix)
            prob = jnp.exp(jnp.where(seen, mul_right(key, query) * scale, NEG) - log_total)
            score = (prob * (mul_right(value, grad) - delta)).astype(jnp.bfloat16)
            dv_ref[there, :] += mul_plain(prob.astype(jnp.bfloat16), grad)
            dk_ref[there, :] += mul_plain(score, query)
            dq_ref[here, :] += mul_left(score, key)
            return carry

        last = jnp.maximum(i + 1, (prefix + BLOCK - 1) // BLOCK)
        return lax.fori_loop(0, jnp.minimum(last, steps), key_step, carry)

    lax.fori_loop(0, steps, query_step, 0)

    def turn_back(values):
        half = HD // 2
        rolled = jnp.concatenate((-values[:, half:], values[:, :half]), axis=1)
        return values * cosine_ref[...] - rolled * sine_ref[...]

    out_ref[:, :HD] = turn_back(dq_ref[...] * scale).astype(jnp.bfloat16)
    out_ref[:, HD : 2 * HD] = turn_back(dk_ref[...] * scale).astype(jnp.bfloat16)
    out_ref[:, 2 * HD :] = dv_ref[...].astype(jnp.bfloat16)


def attention_back(prefix, query, key, value, grad, log_total, delta, cosine, sine):
    span = query.shape[0]
    whole = pl.BlockSpec(memory_space=pltpu.VMEM)
    rows = (span // BLOCK, 1, BLOCK)
    return pl.pallas_call(
        attention_back_kernel,
        out_shape=jax.ShapeDtypeStruct((span, 3 * HD), jnp.bfloat16),
        in_specs=[pl.BlockSpec(memory_space=pltpu.SMEM)] + [whole] * 8,
        out_specs=whole,
        scratch_shapes=[pltpu.VMEM((span, HD), jnp.float32)] * 3,
        compiler_params=pltpu.CompilerParams(vmem_limit_bytes=40 * 2**20),
        cost_estimate=pl.CostEstimate(flops=10**6, bytes_accessed=10**4, transcendentals=0),
    )(
        prefix,
        query,
        key,
        value,
        grad,
        log_total.reshape(rows),
        delta.reshape(rows),
        cosine,
        sine,
    )


def head_split(
    tokens,
    prefix,
    g_attn,
    w_query,
    w_key,
    w_value,
    w_output,
    g_mlp,
    w_gate,
    w_up,
    w_down,
    cotangent,
):
    groups = 8
    tok_rows, width = tokens.shape[1:]
    span = groups * tok_rows
    shard = w_query.shape[0]
    share = w_down.shape[0]
    slice_ff = 4 * share
    per_key = H // KVH
    scale = HD ** (-0.5)
    cut = width // 2

    tok_in = tokens[0].astype(F32)
    gain_one, gain_two = g_attn.astype(F32)[:, None], g_mlp.astype(F32)[:, None]

    q_cols = (gain_one * w_query).astype(BF16).reshape(shard, H, HD)
    k_cols = jnp.repeat((gain_one * w_key).astype(BF16).reshape(shard, KVH, HD), per_key, axis=1)
    v_cols = jnp.repeat((gain_one * w_value).astype(BF16).reshape(shard, KVH, HD), per_key, axis=1)
    qkv_cols = jnp.concatenate((q_cols, k_cols, v_cols), axis=2).transpose(1, 0, 2)

    def gated(weight):
        scaled = (gain_two * weight).astype(BF16).reshape(shard, 4, groups, share)
        return scaled.transpose(2, 0, 1, 3).reshape(groups, shard, slice_ff)

    gate_cols, up_cols = gated(w_gate), gated(w_up)
    cosine, sine = rotary(0, span, HD)

    def turn(values, sine_table):
        half = HD // 2
        rolled = jnp.concatenate((-values[:, half:], values[:, :half]), axis=-1)
        return values * cosine + rolled * sine_table

    down_blocks = send_dp(w_down)
    tok_all = gather(tokens[0], CTX)
    qkv_rows = swap(qkv_cols, CTX).reshape(groups * shard, 3 * HD)
    qkv_rows, out_own, gate_cols, up_cols = join((qkv_rows, w_output, gate_cols, up_cols))
    qkv_blocks = send_dp(qkv_rows)
    out_blocks = [out_own] + send_column(out_own, (1, 2))
    out_blocks += send_column(after(out_own, *qkv_blocks), (3,))
    qkv_w = order_dp(qkv_blocks).reshape(width, 3 * HD)
    out_rows = order_column(out_blocks)
    down_w = order_dp(down_blocks).reshape(slice_ff, width)
    tok_all, qkv_w, down_w, gate_cols, cosine, sine = join(
        (tok_all, qkv_w, down_w, gate_cols, cosine, sine)
    )
    dy_left = gather(after(cotangent[0][:, :cut], tok_all), CTX)
    out_mine = order_dp(send_dp(after(out_rows, qkv_w)))
    gate_rows = swap(gate_cols, CTX).reshape(groups * shard, slice_ff)
    xn_one = normalize(tok_all.astype(F32)).astype(BF16)
    qkv = mul_plain(xn_one, qkv_w)
    query = turn(qkv[:, :HD], sine).astype(BF16)
    key = turn(qkv[:, HD : 2 * HD], sine).astype(BF16)
    value = qkv[:, 2 * HD :].astype(BF16)
    query, key, value, gate_rows, up_cols, out_mine = join(
        (query, key, value, gate_rows, up_cols, out_mine)
    )
    gate_w = gather(gate_rows, ("y", "x"))
    up_rows = swap(up_cols, CTX).reshape(groups * shard, slice_ff)
    scores = mul_right(query, key) * scale
    pos = lax.iota(jnp.int32, span)
    seen = (pos[None, :] <= pos[:, None]) | (pos[None, :] < prefix[0])
    scores = jnp.where(seen, scores, NEG)
    row_max = jnp.max(scores, axis=-1, keepdims=True)
    log_total = row_max + jnp.log(jnp.sum(jnp.exp(scores - row_max), axis=-1, keepdims=True))
    prob_low = jnp.exp(scores - log_total).astype(BF16)
    head_wide = mul_plain(prob_low, value)
    head_o = head_wide.astype(BF16)
    head_o, up_rows = join((head_o, up_rows))
    attn_o = swap(head_o.reshape(groups, tok_rows, HD), CTX)
    output_w = order_cores(out_mine, flip(out_mine, "core")).reshape(H * HD, width)
    attn_o, output_w = join((attn_o, output_w))
    up_blocks = send_dp(up_rows)
    attn_o = attn_o.transpose(1, 0, 2).reshape(tok_rows, H * HD)
    hid_res = tok_in + mul_plain(attn_o, output_w)
    nrm_two = normalize(hid_res)
    xn_two = gather(nrm_two.astype(BF16), CTX)
    up_w = order_dp(up_blocks).reshape(width, slice_ff)
    xn_two, gate_w, up_w, dy_left, dy_own = join(
        (xn_two, gate_w, up_w, dy_left, cotangent[0][:, cut:])
    )
    dy_right = gather(dy_own, CTX)
    gate, up_val = mul_plain(xn_two, gate_w), mul_plain(xn_two, up_w)
    sigmoid_gate = jax.nn.sigmoid(gate)
    hidden = (gate * sigmoid_gate * up_val).astype(BF16)
    mlp_part = mul_plain(hidden, down_w).astype(BF16)
    mlp_part, gate, up_val, dy_right = join((mlp_part, gate, up_val, dy_right))
    mlp_sum = scatter(mlp_part, CTX)
    sigmoid_gate = jax.nn.sigmoid(gate)
    d_hidden = mul_right(dy_left, down_w[:, :cut]) + mul_right(dy_right, down_w[:, cut:])
    d_gate = d_hidden * up_val * sigmoid_gate * (1.0 + gate * (1.0 - sigmoid_gate))
    d_gate = d_gate.astype(BF16)
    d_up = (d_hidden * gate * sigmoid_gate).astype(BF16)

    def by_owner(grad):
        return grad.reshape((4, grad.shape[0] // 4) + grad.shape[1:])

    gate_split = split_parts_dp(by_owner(mul_left(xn_two, d_gate).astype(BF16)))
    up_split = split_parts_dp(by_owner(mul_left(xn_two, d_up).astype(BF16)))
    hidden, d_gate, d_up, gate_split, up_split = join(
        (hidden, d_gate, d_up, gate_split, up_split)
    )
    gate_near = send_parts_dp(gate_split, (1, 2))
    dn_part = (mul_right(d_gate, gate_w) + mul_right(d_up, up_w)).astype(BF16)
    hidden, dn_part, mlp_sum, gate_near, gate_split, up_split = join(
        (hidden, dn_part, mlp_sum, gate_near, gate_split, up_split)
    )
    gate_up_far = send_parts_dp(gate_split, (3,)) + send_parts_dp(up_split)
    dn_two = scatter(dn_part, CTX)
    down_split = [
        split_parts_dp(by_owner(mul_left(hidden, part).astype(BF16))) for part in (dy_left, dy_right)
    ]
    dn_two, gate_up_far, down_split = join((dn_two, gate_up_far, down_split))
    d_res = cotangent[0].astype(F32) + norm_back(hid_res, nrm_two, dn_two)
    d_res_low = d_res.astype(BF16)
    d_attn = mul_right(d_res_low, output_w).astype(BF16)
    d_head = swap(d_attn.reshape(tok_rows, groups, HD).transpose(1, 0, 2), CTX)
    attn_o_two, d_res_two = flip(attn_o, "core"), flip(d_res_low, "core")
    core = lax.axis_index("core")

    def own_columns(values):
        values = values.reshape(tok_rows, 16, 2, shard)
        return lax.dynamic_index_in_dim(values, core, 2, keepdims=False).reshape(tok_rows, -1)

    both_o = jnp.concatenate((own_columns(attn_o), own_columns(attn_o_two)), axis=0)
    both_d = jnp.concatenate((d_res_low, d_res_two), axis=0)
    output_part = mul_left(both_o, both_d).astype(BF16).reshape(4, 4, shard, width)
    output_split = split_parts_dp(output_part)
    gate_parts = gate_split[:1] + gate_near + gate_up_far[:1]
    up_parts = up_split[:1] + gate_up_far[1:]
    gate_up_sum = jnp.stack([add_parts(parts).astype(BF16) for parts in (gate_parts, up_parts)])
    d_head, gate_up_sum, output_split = join((d_head, gate_up_sum, output_split))
    output_parts = output_split[:1] + send_parts_dp(output_split)
    gate_up_sum = gate_up_sum.reshape(2, groups, shard, slice_ff)
    gate_up_sum = lax.all_to_all(gate_up_sum, CTX, split_axis=1, concat_axis=1, tiled=True)
    d_head = d_head.reshape(span, HD)
    row_delta = jnp.sum(d_head.astype(F32) * head_wide, axis=-1)
    d_qkv = attention_back(
        prefix, query, key, value, d_head, log_total, row_delta, cosine, sine
    )
    d_qkv, gate_up_sum, output_parts = join((d_qkv, gate_up_sum, output_parts))
    gate_sum, up_sum = gate_up_sum[0], gate_up_sum[1]
    dn_part_one = mul_right(d_qkv, qkv_w).astype(BF16)
    dn_part_one, xn_one, d_qkv, mlp_sum = join((dn_part_one, xn_one, d_qkv, mlp_sum))
    dn_one = scatter(dn_part_one, CTX)
    result = (hid_res + mlp_sum).astype(BF16)[None]

    qkv_split = split_parts_dp(
        mul_left(xn_one, d_qkv).astype(BF16).reshape(4, groups * shard, 3 * HD)
    )
    qkv_parts = qkv_split[:1] + send_parts_dp(qkv_split)
    column = add_parts(output_parts)
    chip = lax.axis_index(("half", "low"))
    output_parts = [take(column, chip)]
    for step in range(1, 4):
        block = take(column, (chip + step) % 4).astype(BF16)
        output_parts.append(turn_chips(block, step))
    qkv_parts, output_parts, down_split = join((qkv_parts, output_parts, down_split))
    qkv_sum = add_parts(qkv_parts).astype(BF16)
    qkv_sum = swap(qkv_sum.reshape(groups, shard, 3 * HD), CTX)
    output_grad = add_parts(output_parts)
    down_parts = [split[:1] + send_parts_dp(split) for split in down_split]
    down_grad = jnp.concatenate([add_parts(parts) for parts in down_parts], axis=1)

    def ungated(summed):
        blocks = summed.astype(F32).reshape(groups, shard, 4, share)
        return blocks.transpose(1, 2, 0, 3).reshape(shard, FF)

    gate_sum, up_sum = ungated(gate_sum), ungated(up_sum)
    gain_two_grad = jnp.sum(w_gate * gate_sum + w_up * up_sum, axis=1)

    input_grad = d_res + norm_back(tok_in, normalize(tok_in), dn_one)
    input_grad = input_grad.astype(BF16)[None]
    qkv_sum = qkv_sum.astype(F32).transpose(1, 0, 2)
    q_sum = qkv_sum[:, :, :HD].reshape(shard, H * HD)

    def per_group(summed):
        return jnp.sum(summed.reshape(shard, KVH, per_key, HD), axis=2).reshape(shard, KVH * HD)

    k_sum = per_group(qkv_sum[:, :, HD : 2 * HD])
    v_sum = per_group(qkv_sum[:, :, 2 * HD :])
    gain_one_grad = (
        jnp.sum(w_query * q_sum, axis=1)
        + jnp.sum(w_key * k_sum, axis=1)
        + jnp.sum(w_value * v_sum, axis=1)
    )
    return (
        result,
        input_grad,
        gain_one_grad,
        gain_one * q_sum,
        gain_one * k_sum,
        gain_one * v_sum,
        output_grad,
        gain_two_grad,
        gain_two * gate_sum,
        gain_two * up_sum,
        down_grad,
    )


def solution(mesh):
    if dict(mesh.shape) == {"dp": 4, "ctx": 8}:
        body, dp, ctx = head_split, ("y", "x"), CTX
        mesh = Mesh(mesh.devices.reshape(2, 2, 2, 2, 2), dp + ctx)
    else:
        body, dp, ctx = gathered_weights, ("dp",), ("ctx",)
    rows, whole = P(dp + ctx), P(dp + ctx, None)
    acts = P(dp, ctx, None)
    in_specs = (acts, P(dp), rows, whole, whole, whole, whole, rows, whole, whole, whole, acts)
    out_specs = (acts, acts, rows, whole, whole, whole, whole, rows, whole, whole, whole)
    return jax.shard_map(
        body, mesh=mesh, in_specs=in_specs, out_specs=out_specs, check_vma=False
    )
```

```python
import jax
import jax.numpy as jnp
from jax import lax
from jax.experimental import pallas as pl
from jax.experimental.pallas import tpu as pltpu
from jax.sharding import Mesh
from jax.sharding import PartitionSpec as P

FF = 8192
H = 8
KVH = 4
HD = 256
KEYBLK = 512


EPS = 1e-06
THETA = 1000042.0
NEG = -1e30


def mul_plain(first_op, second_op):
    return jnp.dot(first_op, second_op, preferred_element_type=jnp.float32)


def mul_right(first_op, second_op):
    return lax.dot_general(
        first_op, second_op, (((1,), (1,)), ((), ())), preferred_element_type=jnp.float32
    )


def mul_left(first_op, second_op):
    return lax.dot_general(
        first_op, second_op, (((0,), (0,)), ((), ())), preferred_element_type=jnp.float32
    )


def normalize(values):
    return values * lax.rsqrt(jnp.mean(values * values, axis=-1, keepdims=True) + EPS)


def norm_back(values, normed, grad_normed):
    factor = lax.rsqrt(jnp.mean(values * values, axis=-1, keepdims=True) + EPS)
    return factor * (grad_normed - normed * jnp.mean(grad_normed * normed, axis=-1, keepdims=True))


def rotary(first_pos, length, head_dim):
    half_dim = head_dim // 2
    frequency = 1.0 / THETA ** (lax.iota(jnp.float32, half_dim) * (2.0 / head_dim))
    angles = (first_pos + lax.iota(jnp.int32, length)).astype(jnp.float32)[:, None] * frequency[
        None, :
    ]
    cosine = jnp.concatenate((jnp.cos(angles), jnp.cos(angles)), axis=1)
    sine_table = jnp.concatenate((jnp.sin(angles), jnp.sin(angles)), axis=1)
    return (cosine, sine_table)


def rotate(values, cosine, sine_table):
    half_dim = values.shape[-1] // 2
    rolled = jnp.concatenate((-values[..., half_dim:], values[..., :half_dim]), axis=-1)
    return values * cosine[:, None, :] + rolled * sine_table[:, None, :]


def gathered_weights(
    tokens,
    prefix,
    g_attn,
    w_query,
    w_key,
    w_value,
    w_output,
    g_mlp,
    w_gate,
    w_up,
    w_down,
    cotangent,
):
    tok_rows = tokens.shape[1]
    key_span = lax.axis_size("ctx") * tok_rows
    first_pos = lax.axis_index("ctx") * tok_rows
    head_group = H // KVH
    query_width = H * HD
    key_width = KVH * HD
    score_scale = HD ** (-0.5)
    key_blocks = key_span // KEYBLK
    prefix_len = prefix[0]
    tok_in = tokens[0].astype(jnp.float32)
    nrm_one = normalize(tok_in)
    cosine, sine_table = rotary(first_pos, tok_rows, HD)
    query_pos = first_pos + lax.iota(jnp.int32, tok_rows)

    def visible(key_first, length):
        key_pos = key_first + lax.iota(jnp.int32, length)
        return (key_pos[None, :] <= query_pos[:, None]) | (key_pos[None, :] < prefix_len)

    gain_piece = lax.all_gather(g_attn, ("dp", "ctx"), axis=0, tiled=True)
    query_piece = lax.all_gather(w_query, ("dp", "ctx"), axis=0, tiled=True)
    key_piece = lax.all_gather(w_key, ("dp", "ctx"), axis=0, tiled=True)
    value_piece = lax.all_gather(w_value, ("dp", "ctx"), axis=0, tiled=True)
    length = gain_piece.shape[0]
    scaled = (nrm_one * gain_piece.astype(jnp.float32)).astype(jnp.bfloat16)
    q_raw = mul_plain(scaled, query_piece)
    k_raw = mul_plain(scaled, key_piece)
    v_raw = mul_plain(scaled, value_piece)
    xn_one = scaled
    query_low = rotate(q_raw.reshape(tok_rows, H, HD), cosine, sine_table).astype(jnp.bfloat16)
    query_low = query_low.reshape(tok_rows, KVH, head_group, HD)
    key_low = (
        rotate(k_raw.reshape(tok_rows, KVH, HD), cosine, sine_table)
        .astype(jnp.bfloat16)
        .reshape(tok_rows, key_width)
    )
    value_low = v_raw.astype(jnp.bfloat16)
    key_all, value_all = (
        lax.all_gather(key_low, "ctx", axis=0, tiled=True),
        lax.all_gather(value_low, "ctx", axis=0, tiled=True),
    )
    keys_heads = key_all.reshape(key_span, KVH, HD)
    values_heads = value_all.reshape(key_span, KVH, HD)
    scores = (
        jnp.einsum("tkgd,skd->kgts", query_low, keys_heads, preferred_element_type=jnp.float32)
        * score_scale
    )
    scores = jnp.where(visible(0, key_span), scores, NEG)
    row_max = jnp.max(scores, axis=-1, keepdims=True)
    log_total = row_max + jnp.log(jnp.sum(jnp.exp(scores - row_max), axis=-1, keepdims=True))
    prob_low = jnp.exp(scores - log_total).astype(jnp.bfloat16)
    attn_o = jnp.einsum(
        "kgts,skd->tkgd", prob_low, values_heads, preferred_element_type=jnp.float32
    )
    attn_o = attn_o.reshape(tok_rows, query_width).astype(jnp.bfloat16)
    attn_out = mul_plain(attn_o, lax.all_gather(w_output, ("dp", "ctx"), axis=0, tiled=True))
    hid_res = tok_in + attn_out
    nrm_two = normalize(hid_res)
    gain_piece = lax.all_gather(g_mlp, ("dp", "ctx"), axis=0, tiled=True)
    gate_piece = lax.all_gather(w_gate, ("dp", "ctx"), axis=0, tiled=True)
    up_piece = lax.all_gather(w_up, ("dp", "ctx"), axis=0, tiled=True)
    length = gain_piece.shape[0]
    scaled = (nrm_two * gain_piece.astype(jnp.float32)).astype(jnp.bfloat16)
    gate = mul_plain(scaled, gate_piece)
    up_val = mul_plain(scaled, up_piece)
    sigmoid_gate = jax.nn.sigmoid(gate)
    hidden = (gate * sigmoid_gate * up_val).astype(jnp.bfloat16)
    mlp_out = mul_plain(hidden, lax.all_gather(w_down, ("dp", "ctx"), axis=0, tiled=True))
    result = (hid_res + mlp_out).astype(jnp.bfloat16)[None]
    grad_y = cotangent[0]
    grad_hidden = mul_right(grad_y, lax.all_gather(w_down, ("dp", "ctx"), axis=0, tiled=True))
    grad_gate_low = (
        grad_hidden * up_val * sigmoid_gate * (1.0 + gate * (1.0 - sigmoid_gate))
    ).astype(jnp.bfloat16)
    grad_up_low = (grad_hidden * gate * sigmoid_gate).astype(jnp.bfloat16)
    gain_piece = lax.all_gather(g_mlp, ("dp", "ctx"), axis=0, tiled=True)
    gate_piece = lax.all_gather(w_gate, ("dp", "ctx"), axis=0, tiled=True)
    up_piece = lax.all_gather(w_up, ("dp", "ctx"), axis=0, tiled=True)
    summed = mul_right(grad_gate_low, gate_piece) + mul_right(grad_up_low, up_piece)
    stacked = jnp.stack((summed * gain_piece.astype(jnp.float32), summed))
    mlp_pair = stacked
    gain_two_grad = jnp.sum(mlp_pair[1] * nrm_two, axis=0)
    d_res = grad_y.astype(jnp.float32) + norm_back(hid_res, nrm_two, mlp_pair[0])
    gate_up_low = jnp.concatenate((grad_gate_low, grad_up_low), axis=1)
    gate_up_grad = lax.psum_scatter(
        mul_left(scaled, gate_up_low), ("dp", "ctx"), scatter_dimension=0, tiled=True
    )
    down_grad = lax.psum_scatter(
        mul_left(hidden, grad_y), ("dp", "ctx"), scatter_dimension=0, tiled=True
    )
    d_res_low = d_res.astype(jnp.bfloat16)
    grad_attn = mul_right(d_res_low, lax.all_gather(w_output, ("dp", "ctx"), axis=0, tiled=True))
    grad_attn_low = grad_attn.astype(jnp.bfloat16).reshape(tok_rows, KVH, head_group, HD)

    def block_parts(block_id):
        key_first = block_id * KEYBLK
        key_block = lax.dynamic_slice_in_dim(keys_heads, key_first, KEYBLK, 0)
        value_block = lax.dynamic_slice_in_dim(values_heads, key_first, KEYBLK, 0)
        block_scores = (
            jnp.einsum("tkgd,skd->kgts", query_low, key_block, preferred_element_type=jnp.float32)
            * score_scale
        )
        block_scores = jnp.where(visible(key_first, KEYBLK), block_scores, NEG)
        prob_full = jnp.exp(block_scores - log_total)
        grad_prob = jnp.einsum(
            "tkgd,skd->kgts", grad_attn_low, value_block, preferred_element_type=jnp.float32
        )
        return (key_block, prob_full, grad_prob)

    def delta_step(summed, block_id):
        unused_keys, prob_full, grad_prob = block_parts(block_id)
        return (summed + jnp.sum(prob_full * grad_prob, axis=-1, keepdims=True), None)

    row_delta, unused_out = lax.scan(
        delta_step, jnp.zeros(log_total.shape, jnp.float32), lax.iota(jnp.int32, key_blocks)
    )

    def grad_step(grad_query, block_id):
        key_block, prob_full, grad_prob = block_parts(block_id)
        grad_score = (prob_full * (grad_prob - row_delta)).astype(jnp.bfloat16)
        grad_query = (
            grad_query
            + jnp.einsum(
                "kgts,skd->tkgd", grad_score, key_block, preferred_element_type=jnp.float32
            )
            * score_scale
        )
        grad_key_block = (
            jnp.einsum("kgts,tkgd->skd", grad_score, query_low, preferred_element_type=jnp.float32)
            * score_scale
        )
        grad_value_block = jnp.einsum(
            "kgts,tkgd->skd",
            prob_full.astype(jnp.bfloat16),
            grad_attn_low,
            preferred_element_type=jnp.float32,
        )
        return (
            grad_query,
            (
                grad_key_block.reshape(KEYBLK, key_width),
                grad_value_block.reshape(KEYBLK, key_width),
            ),
        )

    grad_query, block_grads = lax.scan(
        grad_step,
        jnp.zeros((tok_rows, KVH, head_group, HD), jnp.float32),
        lax.iota(jnp.int32, key_blocks),
    )
    keys_grad_all = block_grads[0].reshape(key_span, key_width)
    values_grad_all = block_grads[1].reshape(key_span, key_width)
    key_grad_own, value_grad_own = (
        lax.psum_scatter(
            keys_grad_all.astype(jnp.bfloat16), "ctx", scatter_dimension=0, tiled=True
        ).astype(jnp.float32),
        lax.psum_scatter(
            values_grad_all.astype(jnp.bfloat16), "ctx", scatter_dimension=0, tiled=True
        ).astype(jnp.float32),
    )
    query_grad_low = rotate(grad_query.reshape(tok_rows, H, HD), cosine, -sine_table).astype(
        jnp.bfloat16
    )
    query_grad_low = query_grad_low.reshape(tok_rows, query_width)
    key_grad_low = rotate(key_grad_own.reshape(tok_rows, KVH, HD), cosine, -sine_table).astype(
        jnp.bfloat16
    )
    key_grad_low = key_grad_low.reshape(tok_rows, key_width)
    value_grad_low = value_grad_own.astype(jnp.bfloat16)
    gain_piece = lax.all_gather(g_attn, ("dp", "ctx"), axis=0, tiled=True)
    query_piece = lax.all_gather(w_query, ("dp", "ctx"), axis=0, tiled=True)
    key_piece = lax.all_gather(w_key, ("dp", "ctx"), axis=0, tiled=True)
    value_piece = lax.all_gather(w_value, ("dp", "ctx"), axis=0, tiled=True)
    summed = (
        mul_right(query_grad_low, query_piece)
        + mul_right(key_grad_low, key_piece)
        + mul_right(value_grad_low, value_piece)
    )
    stacked = jnp.stack((summed * gain_piece.astype(jnp.float32), summed))
    gain_one_grad = jnp.sum(stacked[1] * nrm_one, axis=0)
    input_grad = (d_res + norm_back(tok_in, nrm_one, stacked[0])).astype(jnp.bfloat16)[None]
    qkv_grad_low = jnp.concatenate((query_grad_low, key_grad_low, value_grad_low), axis=1)
    first_part = mul_left(xn_one, qkv_grad_low)
    second_part = mul_left(attn_o, d_res_low)
    attn_grad = lax.psum_scatter(
        jnp.concatenate((first_part, second_part), axis=1),
        ("dp", "ctx"),
        scatter_dimension=0,
        tiled=True,
    )
    gain_grads = (
        lax.psum_scatter(gain_one_grad, ("dp", "ctx"), scatter_dimension=0, tiled=True),
        lax.psum_scatter(gain_two_grad, ("dp", "ctx"), scatter_dimension=0, tiled=True),
    )
    return (
        result,
        input_grad,
        gain_grads[0],
        attn_grad[:, :query_width],
        attn_grad[:, query_width : query_width + key_width],
        attn_grad[:, query_width + key_width : query_width + 2 * key_width],
        attn_grad[:, query_width + 2 * key_width :],
        gain_grads[1],
        gate_up_grad[:, :FF],
        gate_up_grad[:, FF:],
        down_grad,
    )


BF16, F32 = jnp.bfloat16, jnp.float32
CTX = ("half", "low", "core")
join = lax.optimization_barrier


def put(buffer, block, index):
    return lax.dynamic_update_slice(buffer, block[None], (index,) + (0,) * block.ndim)


def take(values, index):
    return lax.dynamic_index_in_dim(values, index, 0, keepdims=False)


def after(values, *others):
    return join((values,) + others)[0]


def flip(values, axis, bits=1):
    return lax.ppermute(values, axis, [(i, i ^ bits) for i in range(lax.axis_size(axis))])


def send_dp(own):
    return [own] + [flip(own, ("y", "x"), bits) for bits in range(1, 4)]


def order_dp(blocks):
    d = lax.axis_index(("y", "x"))
    buffer = jnp.zeros((4,) + blocks[0].shape, blocks[0].dtype)
    for bits, block in enumerate(blocks):
        buffer = put(buffer, block, d ^ bits)
    return buffer


def split_parts_dp(parts):
    d = lax.axis_index(("y", "x"))
    return [take(parts, d ^ bits) for bits in range(4)]


def send_parts_dp(split, bits=(1, 2, 3)):
    return [flip(split[b], ("y", "x"), b) for b in bits]


def add_parts(parts):
    total = parts[0].astype(F32)
    for part in parts[1:]:
        total = total + part.astype(F32)
    return total


def turn_chips(values, step):
    pairs = [(c, (c + 2 * step) % 8) for c in range(8)]
    return lax.ppermute(values, CTX, pairs)


def send_column(rows, steps=(1, 2, 3)):
    return [turn_chips(rows, step) for step in steps]


def order_column(blocks):
    chip = lax.axis_index(("half", "low"))
    column = jnp.zeros((4,) + blocks[0].shape, blocks[0].dtype)
    for step, block in enumerate(blocks):
        column = put(column, block, (chip - step) % 4)
    return column


def order_cores(mine, other):
    core = lax.axis_index("core")
    low, high = jnp.where(core == 0, mine, other), jnp.where(core == 0, other, mine)
    return jnp.stack((low, high), axis=-3)


def swap(values, axes):
    return lax.all_to_all(values, axes, split_axis=0, concat_axis=0, tiled=True)


def gather(values, axes):
    return lax.all_gather(values, axes, axis=0, tiled=True)


def scatter(values, axes):
    return lax.psum_scatter(values, axes, scatter_dimension=0, tiled=True).astype(F32)


BLOCK = 512


def attention_back_kernel(
    prefix_ref,
    query_ref,
    key_ref,
    value_ref,
    grad_ref,
    log_ref,
    delta_ref,
    cosine_ref,
    sine_ref,
    out_ref,
    dq_ref,
    dk_ref,
    dv_ref,
):
    steps = query_ref.shape[0] // BLOCK
    prefix = prefix_ref[0]
    scale = HD ** (-0.5)
    dq_ref[...] = jnp.zeros_like(dq_ref)
    dk_ref[...] = jnp.zeros_like(dk_ref)
    dv_ref[...] = jnp.zeros_like(dv_ref)
    row = lax.broadcasted_iota(jnp.int32, (BLOCK, BLOCK), 0)
    column = lax.broadcasted_iota(jnp.int32, (BLOCK, BLOCK), 1)

    def query_step(i, carry):
        here = pl.ds(pl.multiple_of(i * BLOCK, BLOCK), BLOCK)
        query, grad = query_ref[here, :], grad_ref[here, :]
        log_total, delta = log_ref[i], delta_ref[i]

        def key_step(j, carry):
            there = pl.ds(pl.multiple_of(j * BLOCK, BLOCK), BLOCK)
            key, value = key_ref[there, :], value_ref[there, :]
            key_pos, query_pos = j * BLOCK + row, i * BLOCK + column
            seen = (key_pos <= query_pos) | (key_pos < prefix)
            prob = jnp.exp(jnp.where(seen, mul_right(key, query) * scale, NEG) - log_total)
            score = (prob * (mul_right(value, grad) - delta)).astype(jnp.bfloat16)
            dv_ref[there, :] += mul_plain(prob.astype(jnp.bfloat16), grad)
            dk_ref[there, :] += mul_plain(score, query)
            dq_ref[here, :] += mul_left(score, key)
            return carry

        last = jnp.maximum(i + 1, (prefix + BLOCK - 1) // BLOCK)
        return lax.fori_loop(0, jnp.minimum(last, steps), key_step, carry)

    lax.fori_loop(0, steps, query_step, 0)

    def turn_back(values):
        half = HD // 2
        rolled = jnp.concatenate((-values[:, half:], values[:, :half]), axis=1)
        return values * cosine_ref[...] - rolled * sine_ref[...]

    out_ref[:, :HD] = turn_back(dq_ref[...] * scale).astype(jnp.bfloat16)
    out_ref[:, HD : 2 * HD] = turn_back(dk_ref[...] * scale).astype(jnp.bfloat16)
    out_ref[:, 2 * HD :] = dv_ref[...].astype(jnp.bfloat16)


def attention_back(prefix, query, key, value, grad, log_total, delta, cosine, sine):
    span = query.shape[0]
    whole = pl.BlockSpec(memory_space=pltpu.VMEM)
    rows = (span // BLOCK, 1, BLOCK)
    return pl.pallas_call(
        attention_back_kernel,
        out_shape=jax.ShapeDtypeStruct((span, 3 * HD), jnp.bfloat16),
        in_specs=[pl.BlockSpec(memory_space=pltpu.SMEM)] + [whole] * 8,
        out_specs=whole,
        scratch_shapes=[pltpu.VMEM((span, HD), jnp.float32)] * 3,
        compiler_params=pltpu.CompilerParams(vmem_limit_bytes=40 * 2**20),
        cost_estimate=pl.CostEstimate(flops=10**6, bytes_accessed=10**4, transcendentals=0),
    )(
        prefix,
        query,
        key,
        value,
        grad,
        log_total.reshape(rows),
        delta.reshape(rows),
        cosine,
        sine,
    )


def head_split(
    tokens,
    prefix,
    g_attn,
    w_query,
    w_key,
    w_value,
    w_output,
    g_mlp,
    w_gate,
    w_up,
    w_down,
    cotangent,
):
    groups = 8
    tok_rows, width = tokens.shape[1:]
    span = groups * tok_rows
    shard = w_query.shape[0]
    share = w_down.shape[0]
    slice_ff = 4 * share
    per_key = H // KVH
    scale = HD ** (-0.5)
    cut = width // 2

    tok_in = tokens[0].astype(F32)
    gain_one, gain_two = g_attn.astype(F32)[:, None], g_mlp.astype(F32)[:, None]

    q_cols = (gain_one * w_query).astype(BF16).reshape(shard, H, HD)
    k_cols = jnp.repeat((gain_one * w_key).astype(BF16).reshape(shard, KVH, HD), per_key, axis=1)
    v_cols = jnp.repeat((gain_one * w_value).astype(BF16).reshape(shard, KVH, HD), per_key, axis=1)
    qkv_cols = jnp.concatenate((q_cols, k_cols, v_cols), axis=2).transpose(1, 0, 2)

    def gated(weight):
        scaled = (gain_two * weight).astype(BF16).reshape(shard, 4, groups, share)
        return scaled.transpose(2, 0, 1, 3).reshape(groups, shard, slice_ff)

    gate_cols, up_cols = gated(w_gate), gated(w_up)
    cosine, sine = rotary(0, span, HD)

    def turn(values, sine_table):
        half = HD // 2
        rolled = jnp.concatenate((-values[:, half:], values[:, :half]), axis=-1)
        return values * cosine + rolled * sine_table

    down_blocks = send_dp(w_down)
    tok_all = gather(tokens[0], CTX)
    qkv_rows = swap(qkv_cols, CTX).reshape(groups * shard, 3 * HD)
    qkv_rows, out_own, gate_cols, up_cols = join((qkv_rows, w_output, gate_cols, up_cols))
    qkv_blocks = send_dp(qkv_rows)
    out_blocks = [out_own] + send_column(out_own, (1, 2))
    out_blocks += send_column(after(out_own, *qkv_blocks), (3,))
    qkv_w = order_dp(qkv_blocks).reshape(width, 3 * HD)
    out_rows = order_column(out_blocks)
    down_w = order_dp(down_blocks).reshape(slice_ff, width)
    tok_all, qkv_w, down_w, gate_cols, cosine, sine = join(
        (tok_all, qkv_w, down_w, gate_cols, cosine, sine)
    )
    dy_left = gather(after(cotangent[0][:, :cut], tok_all), CTX)
    out_mine = order_dp(send_dp(after(out_rows, qkv_w)))
    gate_rows = swap(gate_cols, CTX).reshape(groups * shard, slice_ff)
    xn_one = normalize(tok_all.astype(F32)).astype(BF16)
    qkv = mul_plain(xn_one, qkv_w)
    query = turn(qkv[:, :HD], sine).astype(BF16)
    key = turn(qkv[:, HD : 2 * HD], sine).astype(BF16)
    value = qkv[:, 2 * HD :].astype(BF16)
    query, key, value, gate_rows, up_cols, out_mine = join(
        (query, key, value, gate_rows, up_cols, out_mine)
    )
    gate_w = gather(gate_rows, ("y", "x"))
    up_rows = swap(up_cols, CTX).reshape(groups * shard, slice_ff)
    scores = mul_right(query, key) * scale
    pos = lax.iota(jnp.int32, span)
    seen = (pos[None, :] <= pos[:, None]) | (pos[None, :] < prefix[0])
    scores = jnp.where(seen, scores, NEG)
    row_max = jnp.max(scores, axis=-1, keepdims=True)
    log_total = row_max + jnp.log(jnp.sum(jnp.exp(scores - row_max), axis=-1, keepdims=True))
    prob_low = jnp.exp(scores - log_total).astype(BF16)
    head_wide = mul_plain(prob_low, value)
    head_o = head_wide.astype(BF16)
    head_o, up_rows = join((head_o, up_rows))
    attn_o = swap(head_o.reshape(groups, tok_rows, HD), CTX)
    output_w = order_cores(out_mine, flip(out_mine, "core")).reshape(H * HD, width)
    attn_o, output_w = join((attn_o, output_w))
    up_blocks = send_dp(up_rows)
    attn_o = attn_o.transpose(1, 0, 2).reshape(tok_rows, H * HD)
    hid_res = tok_in + mul_plain(attn_o, output_w)
    nrm_two = normalize(hid_res)
    xn_two = gather(nrm_two.astype(BF16), CTX)
    up_w = order_dp(up_blocks).reshape(width, slice_ff)
    xn_two, gate_w, up_w, dy_left, dy_own = join(
        (xn_two, gate_w, up_w, dy_left, cotangent[0][:, cut:])
    )
    dy_right = gather(dy_own, CTX)
    gate, up_val = mul_plain(xn_two, gate_w), mul_plain(xn_two, up_w)
    sigmoid_gate = jax.nn.sigmoid(gate)
    hidden = (gate * sigmoid_gate * up_val).astype(BF16)
    mlp_part = mul_plain(hidden, down_w).astype(BF16)
    mlp_part, gate, up_val, dy_right = join((mlp_part, gate, up_val, dy_right))
    mlp_sum = scatter(mlp_part, CTX)
    sigmoid_gate = jax.nn.sigmoid(gate)
    d_hidden = mul_right(dy_left, down_w[:, :cut]) + mul_right(dy_right, down_w[:, cut:])
    d_gate = d_hidden * up_val * sigmoid_gate * (1.0 + gate * (1.0 - sigmoid_gate))
    d_gate = d_gate.astype(BF16)
    d_up = (d_hidden * gate * sigmoid_gate).astype(BF16)

    def by_owner(grad):
        return grad.reshape((4, grad.shape[0] // 4) + grad.shape[1:])

    gate_split = split_parts_dp(by_owner(mul_left(xn_two, d_gate).astype(BF16)))
    up_split = split_parts_dp(by_owner(mul_left(xn_two, d_up).astype(BF16)))
    hidden, d_gate, d_up, gate_split, up_split = join(
        (hidden, d_gate, d_up, gate_split, up_split)
    )
    gate_near = send_parts_dp(gate_split, (1, 2))
    dn_part = (mul_right(d_gate, gate_w) + mul_right(d_up, up_w)).astype(BF16)
    hidden, dn_part, mlp_sum, gate_near, gate_split, up_split = join(
        (hidden, dn_part, mlp_sum, gate_near, gate_split, up_split)
    )
    gate_up_far = send_parts_dp(gate_split, (3,)) + send_parts_dp(up_split)
    dn_two = scatter(dn_part, CTX)
    down_split = [
        split_parts_dp(by_owner(mul_left(hidden, part).astype(BF16))) for part in (dy_left, dy_right)
    ]
    dn_two, gate_up_far, down_split = join((dn_two, gate_up_far, down_split))
    d_res = cotangent[0].astype(F32) + norm_back(hid_res, nrm_two, dn_two)
    d_res_low = d_res.astype(BF16)
    d_attn = mul_right(d_res_low, output_w).astype(BF16)
    d_head = swap(d_attn.reshape(tok_rows, groups, HD).transpose(1, 0, 2), CTX)
    attn_o_two, d_res_two = flip(attn_o, "core"), flip(d_res_low, "core")
    core = lax.axis_index("core")

    def own_columns(values):
        values = values.reshape(tok_rows, 16, 2, shard)
        return lax.dynamic_index_in_dim(values, core, 2, keepdims=False).reshape(tok_rows, -1)

    both_o = jnp.concatenate((own_columns(attn_o), own_columns(attn_o_two)), axis=0)
    both_d = jnp.concatenate((d_res_low, d_res_two), axis=0)
    output_part = mul_left(both_o, both_d).astype(BF16).reshape(4, 4, shard, width)
    output_split = split_parts_dp(output_part)
    gate_parts = gate_split[:1] + gate_near + gate_up_far[:1]
    up_parts = up_split[:1] + gate_up_far[1:]
    gate_up_sum = jnp.stack([add_parts(parts).astype(BF16) for parts in (gate_parts, up_parts)])
    d_head, gate_up_sum, output_split = join((d_head, gate_up_sum, output_split))
    output_parts = output_split[:1] + send_parts_dp(output_split)
    gate_up_sum = gate_up_sum.reshape(2, groups, shard, slice_ff)
    gate_up_sum = lax.all_to_all(gate_up_sum, CTX, split_axis=1, concat_axis=1, tiled=True)
    d_head = d_head.reshape(span, HD)
    row_delta = jnp.sum(d_head.astype(F32) * head_wide, axis=-1)
    d_qkv = attention_back(
        prefix, query, key, value, d_head, log_total, row_delta, cosine, sine
    )
    qkv_split = split_parts_dp(
        mul_left(xn_one, d_qkv).astype(BF16).reshape(4, groups * shard, 3 * HD)
    )
    d_qkv, gate_up_sum, output_parts, qkv_split = join(
        (d_qkv, gate_up_sum, output_parts, qkv_split)
    )
    gate_sum, up_sum = gate_up_sum[0], gate_up_sum[1]
    dn_part_one = mul_right(d_qkv, qkv_w).astype(BF16)
    dn_part_one, mlp_sum = join((dn_part_one, mlp_sum))
    dn_one = scatter(dn_part_one, CTX)
    result = (hid_res + mlp_sum).astype(BF16)[None]
    qkv_parts = qkv_split[:1] + send_parts_dp(qkv_split)
    column = add_parts(output_parts)
    chip = lax.axis_index(("half", "low"))
    output_parts = [take(column, chip)]
    for step in range(1, 4):
        block = take(column, (chip + step) % 4).astype(BF16)
        output_parts.append(turn_chips(block, step))
    qkv_parts, output_parts, down_split = join((qkv_parts, output_parts, down_split))
    qkv_sum = add_parts(qkv_parts).astype(BF16)
    qkv_sum = swap(qkv_sum.reshape(groups, shard, 3 * HD), CTX)
    output_grad = add_parts(output_parts)
    down_parts = [split[:1] + send_parts_dp(split) for split in down_split]
    down_grad = jnp.concatenate([add_parts(parts) for parts in down_parts], axis=1)

    def ungated(summed):
        blocks = summed.astype(F32).reshape(groups, shard, 4, share)
        return blocks.transpose(1, 2, 0, 3).reshape(shard, FF)

    gate_sum, up_sum = ungated(gate_sum), ungated(up_sum)
    gain_two_grad = jnp.sum(w_gate * gate_sum + w_up * up_sum, axis=1)

    input_grad = d_res + norm_back(tok_in, normalize(tok_in), dn_one)
    input_grad = input_grad.astype(BF16)[None]
    qkv_sum = qkv_sum.astype(F32).transpose(1, 0, 2)
    q_sum = qkv_sum[:, :, :HD].reshape(shard, H * HD)

    def per_group(summed):
        return jnp.sum(summed.reshape(shard, KVH, per_key, HD), axis=2).reshape(shard, KVH * HD)

    k_sum = per_group(qkv_sum[:, :, HD : 2 * HD])
    v_sum = per_group(qkv_sum[:, :, 2 * HD :])
    gain_one_grad = (
        jnp.sum(w_query * q_sum, axis=1)
        + jnp.sum(w_key * k_sum, axis=1)
        + jnp.sum(w_value * v_sum, axis=1)
    )
    return (
        result,
        input_grad,
        gain_one_grad,
        gain_one * q_sum,
        gain_one * k_sum,
        gain_one * v_sum,
        output_grad,
        gain_two_grad,
        gain_two * gate_sum,
        gain_two * up_sum,
        down_grad,
    )


def solution(mesh):
    if dict(mesh.shape) == {"dp": 4, "ctx": 8}:
        body, dp, ctx = head_split, ("y", "x"), CTX
        mesh = Mesh(mesh.devices.reshape(2, 2, 2, 2, 2), dp + ctx)
    else:
        body, dp, ctx = gathered_weights, ("dp",), ("ctx",)
    rows, whole = P(dp + ctx), P(dp + ctx, None)
    acts = P(dp, ctx, None)
    in_specs = (acts, P(dp), rows, whole, whole, whole, whole, rows, whole, whole, whole, acts)
    out_specs = (acts, acts, rows, whole, whole, whole, whole, rows, whole, whole, whole)
    return jax.shard_map(
        body, mesh=mesh, in_specs=in_specs, out_specs=out_specs, check_vma=False
    )
```
